128 devices in a mesh: tm: 8 (over y_lo, x), slab: 16 (over y_hi, z, core).
Axes of the slice: x: 4, y: 4 (y_hi: 2, y_lo: 2; y = y_hi * 2 + y_lo), z: 4, core: 2. Of those that a mesh axis runs over, the one named last changes fastest.
Arguments:
- u_states: bfloat16 [8, 64, 64, 8, 256], P('tm', None, 'slab'), may hold values from -6 to 6
- lam_points: float32 [8, 64, 64, 8, 256], P('tm', None, 'slab'), may hold values from -6 to 6
- weight: bfloat16 [27, 64, 64], replicated, may hold values from -0.15625 to 0.15625
- bias: float32 [64], replicated, may hold values from -3 to 3
Outputs:
- lam_new: float32 [8, 64, 64, 8, 256], P('tm', None, 'slab')
- grad_w: float32 [27, 64, 64], replicated
- grad_b: float32 [64], replicated
The draws below stay inside these ranges and needn't reach their ends.
All inputs are finite; a program needn't handle non-finite values.
Results may differ from the reference program's by a relative error of at most 0.0065.
Values may be sent and summed in bfloat16 or wider, within the bound.
No kernel may reach another device: no remote copies, remote signals or barrier semaphores. Data moves between devices by JAX's collectives and lax.ppermute only.
A program may use at most 256 MiB of HBM per device.

```python
import math
from functools import partial
import jax
import jax.numpy as jnp
from jax import lax

C = 64
CX = 8
CY = 256
GROUPS = 8
NZ = 64
N_TM = 8


def shard_levels(stream_key, shape, shards, low, high):
    loudness = 1.0
    for dim, parts in shards:
        steps = jax.random.uniform(jax.random.fold_in(jax.random.fold_in(stream_key, 6), dim), (parts,), jnp.float32, low / len(shards), high / len(shards))
        loudness = loudness * jnp.repeat(jnp.exp(steps), shape[dim] // parts).reshape((-1,) + (1,) * (len(shape) - 1 - dim))
    return loudness


def noise(rng, dims, spread, limit, cuts=(), kind=jnp.bfloat16):
    entries = spread * jax.random.normal(rng, dims, jnp.float32)
    if cuts:
        entries = entries * shard_levels(rng, dims, cuts, -0.22, 0.18)
    return jnp.clip(entries, -limit, limit).astype(kind)


def setup_inputs(seed: int = 0) -> dict:
    arg_keys = jax.random.split(jax.random.key(seed), 5)
    return {
        "u_states": noise(arg_keys[0], (GROUPS, C, NZ, CX, CY), 1.0, 6.0, ((0, 8), (2, 16))),
        "lam_points": noise(arg_keys[1], (GROUPS, C, NZ, CX, CY), 1.0, 6.0, ((0, 8), (2, 16)), jnp.float32),
        "weight": noise(arg_keys[2], (27, C, C), (27 * C) ** -0.5, 0.15625),
        "bias": noise(arg_keys[3], (C,), 0.5, 3.0, (), jnp.float32),
    }


step_size = 0.25

def correlate(field, kernel):
    return lax.conv_general_dilated(field[None], kernel, (1, 1, 1), ((1, 1), (1, 1), (1, 1)), dimension_numbers=('NCDHW', 'OIDHW', 'NCDHW'), precision=lax.Precision.HIGHEST)[0]

def restrict(field):
    shaped = field.reshape(field.shape[0], field.shape[1], field.shape[2] // 2, 2, field.shape[3] // 2, 2)
    return lax.optimization_barrier(jnp.mean(shaped, axis=(3, 5)))

def prolong(field):
    return jnp.repeat(jnp.repeat(field, 2, axis=2), 2, axis=3)

def rounded(value):
    return lax.optimization_barrier(value.astype(jnp.bfloat16)).astype(jnp.float32)

def group_pass(kernel, bias, diagonal, inputs):
    state_zero, adjoint = inputs
    offset = bias[:, None, None, None]
    start = state_zero.astype(jnp.float32)
    tanh_zero = jnp.tanh(correlate(start, kernel) + offset)
    sens_zero = 1.0 - tanh_zero * tanh_zero
    state_one = rounded(start + step_size * tanh_zero)
    tanh_one = jnp.tanh(correlate(state_one, kernel) + offset)
    sens_one = 1.0 - tanh_one * tanh_one
    cot_one = rounded(sens_one * adjoint)
    _, pull_one = jax.vjp(correlate, state_one, kernel)
    back_one, kgrad_one = pull_one(cot_one)
    middle = adjoint + step_size * back_one
    cot_zero = rounded(sens_zero * middle)
    _, pull_zero = jax.vjp(correlate, start, kernel)
    back_zero, kgrad_zero = pull_zero(cot_zero)
    fine_back = middle + step_size * back_zero
    factor = 1.0 + 2.0 * step_size * diagonal[:, None, None, None] * restrict(sens_zero)
    bias_grad = lax.optimization_barrier(jnp.sum(cot_zero + cot_one, axis=(1, 2, 3)))
    return (restrict(fine_back), factor, kgrad_zero + kgrad_one, bias_grad)

def descend(earlier, inputs):
    value = inputs[0] * earlier + inputs[1]
    return (value, value)

def reference(u_states, lam_points, weight, bias):
    kernel = weight.astype(jnp.float32).reshape(3, 3, 3, C, C).transpose(3, 4, 0, 1, 2)
    diagonal = jnp.diagonal(weight[13]).astype(jnp.float32)
    coarse_back, factor, kgrad, bias_grad = lax.map(partial(group_pass, kernel, bias, diagonal), (u_states, lam_points))
    zero_block = jnp.zeros_like(coarse_back[:1])
    rest = jnp.concatenate([zero_block, coarse_back[:-1]], 0) - jax.vmap(restrict)(lam_points)
    factor_prev = jnp.concatenate([zero_block, factor[:-1]], 0)
    _, correction = lax.scan(descend, jnp.zeros_like(rest[0]), (factor_prev, rest))
    lam_new = lam_points + jax.vmap(prolong)(correction)
    grad_scale = step_size / math.sqrt(2 * N_TM * NZ * CX * CY)
    grad_w = grad_scale * lax.optimization_barrier(jnp.sum(kgrad, 0)).transpose(2, 3, 4, 0, 1).reshape(27, C, C)
    grad_b = grad_scale * lax.optimization_barrier(jnp.sum(bias_grad, 0))
    return (lam_new, grad_w, grad_b)
```

```python
import functools
import math

import jax
import jax.numpy as jnp
from jax import lax
from jax.experimental import pallas as pl
from jax.experimental.pallas import tpu as pltpu
from jax.sharding import PartitionSpec as P

f32, bf16 = jnp.float32, jnp.bfloat16
STEP = 0.25
VMEM_LIMIT = 56 * 2**20
PARAMS = pltpu.CompilerParams(vmem_limit_bytes=VMEM_LIMIT)


def shifts(value):
    lane = lax.broadcasted_iota(jnp.int32, value.shape, 1)
    zero = jnp.zeros((), value.dtype)
    left = jnp.where(lane == 0, zero, pltpu.roll(value, 1, 1))
    right = jnp.where(lane == 255, zero, pltpu.roll(value, 255, 1))
    return left, right


def put(wide, plane, row, pair, value):
    count = value.shape[0]
    left, right = shifts(value)
    base = plane * 384 + row
    cols = slice(pair * 256, pair * 256 + 256)
    wide[pl.ds(base, count), cols] = left
    wide[pl.ds(base + 128, count), cols] = value
    wide[pl.ds(base + 256, count), cols] = right


def to_rows(source, z, turn):
    value = source[:, z].astype(f32).reshape(512, 256)
    turn[0] = value[:, :128]
    turn[1] = value[:, 128:]


def row_of(turn, x):
    return jnp.concatenate([turn[half, pl.ds(x, 64, stride=8), :] for half in range(2)], 1)


def pair_of(turn, pair):
    return jnp.concatenate([row_of(turn, 2 * pair), row_of(turn, 2 * pair + 1)], 0)


def products(matrix, wide, z):
    base = pl.multiple_of(z * 384, 384)
    return [
        jnp.dot(
            matrix[...],
            wide[pl.ds(base, 1152), pair * 256 : pair * 256 + 256],
            preferred_element_type=f32,
        )
        for pair in range(4)
    ]


def combined(parts, pair):
    low, high = parts[pair][0:64], parts[pair][64:128]
    if pair > 0:
        low = low + parts[pair - 1][192:256]
    if pair < 3:
        high = high + parts[pair + 1][128:192]
    return jnp.concatenate([low, high], 0)


def averaging():
    fine = lax.broadcasted_iota(jnp.int32, (256, 128), 0)
    coarse = lax.broadcasted_iota(jnp.int32, (256, 128), 1)
    return jnp.where((fine == 2 * coarse) | (fine == 2 * coarse + 1), 0.25, 0.0).astype(bf16)


def split_dot(value, matrix):
    high = value.astype(bf16)
    low = (value - high.astype(f32)).astype(bf16)
    return jnp.dot(high, matrix, preferred_element_type=f32) + jnp.dot(
        low, matrix, preferred_element_type=f32
    )


def forward_body(mask, u, u_lo, u_hi, lam, matrix, bias, diag, cot, sens, state, start, factor, wide0, wide1, turn):
    for z in range(8):
        source, place = ((u_lo, z), (u, z - 2), (u_hi, z - 6))[(z >= 2) + (z >= 6)]
        to_rows(source, place, turn)
        for pair in range(4):
            value = pair_of(turn, pair).astype(bf16)
            put(wide0, z, 0, pair, value)
            if 1 <= z <= 6:
                start[z - 1, :, pair * 256 : pair * 256 + 256] = value
    offset = bias[...]

    def first(z, carry):
        parts = products(matrix, wide0, z)
        for pair in range(4):
            cols = slice(pair * 256, pair * 256 + 256)
            tanh = jnp.tanh(combined(parts, pair) + offset)
            sens[z, :, cols] = 1.0 - tanh * tanh
            value = (start[z, :, cols].astype(f32) + STEP * tanh) * mask[z]
            value = value.astype(bf16)
            state[z, :, cols] = value
            put(wide1, z, 0, pair, value)
        return carry

    lax.fori_loop(0, 6, first, 0)
    average = averaging()

    def second(z, carry):
        parts = products(matrix, wide1, z)
        to_rows(lam, z, turn)
        for pair in range(4):
            cols = slice(pair * 256, pair * 256 + 256)
            tanh = jnp.tanh(combined(parts, pair) + offset)
            cot[z, :, cols] = ((1.0 - tanh * tanh) * pair_of(turn, pair)).astype(bf16)
            both = sens[z + 1, 0:64, cols] + sens[z + 1, 64:128, cols]
            coarse = jnp.dot(both.astype(bf16), average, preferred_element_type=f32)
            factor[z, pair] = (coarse * diag[...]).astype(bf16)
        return carry

    lax.fori_loop(0, 4, second, 0)


def forward(mask, u, u_lo, u_hi, lam, matrix, bias, diag):
    vmem = pl.BlockSpec(memory_space=pltpu.VMEM)
    return pl.pallas_call(
        forward_body,
        out_shape=(
            jax.ShapeDtypeStruct((4, 128, 1024), bf16),
            jax.ShapeDtypeStruct((6, 128, 1024), f32),
            jax.ShapeDtypeStruct((6, 128, 1024), bf16),
            jax.ShapeDtypeStruct((6, 128, 1024), bf16),
            jax.ShapeDtypeStruct((4, 4, 64, 128), bf16),
        ),
        in_specs=[pl.BlockSpec(memory_space=pltpu.SMEM)] + [vmem] * 7,
        scratch_shapes=[
            pltpu.VMEM((8 * 384, 1024), bf16),
            pltpu.VMEM((6 * 384, 1024), bf16),
            pltpu.VMEM((2, 512, 128), f32),
        ],
        compiler_params=PARAMS,
        name="forward",
    )(mask, u, u_lo, u_hi, lam, matrix, bias, diag)


def backward_body(mask, cot1, cot_lo, cot_hi, lam, lam_lo, lam_hi, sens, matrix, factor, cot0, coarse, average_lam, wide1, wide0, middle, turn):
    for z in range(8):
        source, place = ((cot_lo, z), (cot1, z - 2), (cot_hi, z - 6))[(z >= 2) + (z >= 6)]
        for pair in range(4):
            put(wide1, z, 0, pair, source[place, :, pair * 256 : pair * 256 + 256])

    def first(z, source, place):
        parts = products(matrix, wide1, z)
        to_rows(source, place, turn)
        for pair in range(4):
            cols = slice(pair * 256, pair * 256 + 256)
            value = pair_of(turn, pair) + STEP * combined(parts, pair)
            middle[z, :, cols] = value
            value = (sens[z, :, cols] * value * mask[z]).astype(bf16)
            put(wide0, z, 0, pair, value)
            if source is lam:
                cot0[place, :, cols] = value

    def inner(z, carry):
        first(z + 1, lam, z)
        return carry

    first(0, lam_lo, 0)
    lax.fori_loop(0, 4, inner, 0)
    first(5, lam_hi, 0)
    average = averaging()

    def second(z, carry):
        parts = products(matrix, wide0, z)
        to_rows(lam, z, turn)
        for pair in range(4):
            cols = slice(pair * 256, pair * 256 + 256)
            value = middle[z + 1, :, cols] + STEP * combined(parts, pair)
            back = split_dot(value[0:64] + value[64:128], average)
            here = split_dot(row_of(turn, 2 * pair) + row_of(turn, 2 * pair + 1), average)
            average_lam[z, pair] = here
            coarse[z, pair] = (back - here - factor[z, pair].astype(f32) * here).astype(bf16)
        return carry

    lax.fori_loop(0, 4, second, 0)


def backward(mask, cot1, cot_lo, cot_hi, lam, lam_lo, lam_hi, sens, matrix, factor):
    vmem = pl.BlockSpec(memory_space=pltpu.VMEM)
    return pl.pallas_call(
        backward_body,
        out_shape=(
            jax.ShapeDtypeStruct((4, 128, 1024), bf16),
            jax.ShapeDtypeStruct((4, 4, 64, 128), bf16),
            jax.ShapeDtypeStruct((4, 4, 64, 128), f32),
        ),
        in_specs=[pl.BlockSpec(memory_space=pltpu.SMEM)] + [vmem] * 9,
        scratch_shapes=[
            pltpu.VMEM((8 * 384, 1024), bf16),
            pltpu.VMEM((6 * 384, 1024), bf16),
            pltpu.VMEM((6, 128, 1024), f32),
            pltpu.VMEM((2, 512, 128), f32),
        ],
        compiler_params=PARAMS,
        name="backward",
    )(mask, cot1, cot_lo, cot_hi, lam, lam_lo, lam_hi, sens, matrix, factor)


def gradient_body(scale, cot, state, *refs):
    earlier = refs[0] if len(refs) == 5 else None
    out, wide, widened_cot, total = refs[-4:]
    for z in range(6):
        for pair in range(4):
            put(wide, z, 0, pair, state[z, :, pair * 256 : pair * 256 + 256])
    sums = jnp.zeros((128, 128), f32)
    zero = jnp.zeros((64, 256), bf16)
    for z in range(4):
        value = cot[z]
        widened_cot[z, 0:128] = value
        widened_cot[z, 128:192] = jnp.concatenate([zero, value[64:128, :768]], 1)
        widened_cot[z, 192:256] = jnp.concatenate([value[0:64, 256:], zero], 1)
        for part in range(8):
            sums = sums + value[:, part * 128 : part * 128 + 128].astype(f32)
    total[...] = jnp.zeros_like(total)

    def plane(z, carry):
        base = pl.multiple_of(z * 384, 384)
        total[...] += lax.dot_general(
            widened_cot[z],
            wide[pl.ds(base, 1152), :],
            (((1,), (1,)), ((), ())),
            preferred_element_type=f32,
        )
        return carry

    lax.fori_loop(0, 4, plane, 0)
    lower = lax.broadcasted_iota(jnp.int32, (64, 128), 1) < 64

    def give(block, value):
        value = value * scale
        out[block] = value if earlier is None else value + earlier[block]

    for tap in range(9):
        cols = slice(tap * 128, tap * 128 + 128)
        rows = [total[64 * q : 64 * q + 64, cols] for q in range(4)]
        taps = [jnp.where(lower, rows[1], rows[3]), jnp.where(lower, rows[0], rows[1]), jnp.where(lower, rows[2], rows[0])]
        taps = [value + pltpu.roll(value, 64, 1) for value in taps]
        give(tap, jnp.where(lower, taps[0], taps[1]))
        if tap % 2 == 0:
            kept = taps[2]
        else:
            give(9 + tap // 2, jnp.where(lower, kept, taps[2]))
    give(13, kept)
    give(14, sums[0:64] + sums[64:128])
    give(15, jnp.zeros((64, 128), f32))


def gradient(scale, cot, state, earlier=None):
    return pl.pallas_call(
        functools.partial(gradient_body, scale),
        out_shape=jax.ShapeDtypeStruct((16, 64, 128), f32),
        scratch_shapes=[
            pltpu.VMEM((6 * 384, 1024), bf16),
            pltpu.VMEM((4, 256, 1024), bf16),
            pltpu.VMEM((256, 1152), f32),
        ],
        compiler_params=PARAMS,
        name="gradient",
    )(*((cot, state) if earlier is None else (cot, state, earlier)))


def taps_body(summed, out):
    for a in range(3):
        for c in range(3):
            tap = 3 * a + c
            out[9 * a + c] = summed[tap][:, :64]
            out[9 * a + 3 + c] = summed[tap][:, 64:]
            half = 64 * (tap % 2)
            out[9 * a + 6 + c] = summed[9 + tap // 2][:, half : half + 64]


def taps_of(summed):
    return pl.pallas_call(
        taps_body,
        out_shape=jax.ShapeDtypeStruct((27, 64, 64), f32),
        compiler_params=PARAMS,
        name="taps",
    )(summed)


def sweep_body(factor, coarse, out):
    value = jnp.zeros(coarse.shape[1:], f32)
    out[0] = value.astype(bf16)
    for group in range(coarse.shape[0] - 1):
        value = value + factor[group].astype(f32) * value + coarse[group].astype(f32)
        out[group + 1] = value.astype(bf16)


def sweep(factor, coarse):
    return pl.pallas_call(
        sweep_body,
        out_shape=jax.ShapeDtypeStruct(coarse.shape, bf16),
        compiler_params=PARAMS,
        name="sweep",
    )(factor, coarse)


def finish_body(lam, average_lam, carried, out, turn):
    fine = lax.broadcasted_iota(jnp.int32, (128, 256), 1)
    coarse = lax.broadcasted_iota(jnp.int32, (128, 256), 0)
    copies = jnp.where((fine == 2 * coarse) | (fine == 2 * coarse + 1), 1.0, 0.0).astype(bf16)

    def plane(z, carry):
        for pair in range(4):
            value = split_dot(carried[z, pair].astype(f32) - average_lam[z, pair], copies)
            for half in range(2):
                for x in (2 * pair, 2 * pair + 1):
                    turn[half, pl.ds(x, 64, stride=8), :] = value[:, half * 128 : half * 128 + 128]
        added = jnp.concatenate([turn[0], turn[1]], 1).reshape(64, 8, 256)
        out[:, z] = lam[:, z] + added
        return carry

    lax.fori_loop(0, 4, plane, 0)


def finish(lam, average_lam, carried):
    return pl.pallas_call(
        finish_body,
        out_shape=jax.ShapeDtypeStruct((64, 4, 8, 256), f32),
        scratch_shapes=[pltpu.VMEM((2, 512, 128), f32)],
        compiler_params=PARAMS,
        name="finish",
    )(lam, average_lam, carried)


def tap_matrix(weight):
    taps = weight.reshape(3, 3, 3, 64, 64).transpose(1, 3, 0, 2, 4)
    none = jnp.zeros_like(taps[0])
    even = jnp.stack([taps[1], taps[0], taps[2], none])
    odd = jnp.stack([taps[2], taps[1], none, taps[0]])
    return jnp.stack([even, odd], 4).reshape(256, 1152)


def neighbours(low_part, high_part):
    count = lax.axis_size("slab")
    up = [(i, i + 1) for i in range(count - 1)]
    down = [(i + 1, i) for i in range(count - 1)]
    return lax.ppermute(high_part, "slab", up), lax.ppermute(low_part, "slab", down)


def exchanged(value, axes):
    return lax.all_to_all(value, axes, 0, 0, tiled=True)


def on_device(u_states, lam_points, weight, bias):
    u, lam = u_states[0], lam_points[0]
    slab, slabs = lax.axis_index("slab"), lax.axis_size("slab")
    devices = slabs * lax.axis_size("tm")
    u_lo, u_hi = neighbours(u[:, :2], u[:, 2:])
    lam_lo, lam_hi = neighbours(lam[:, :1].astype(bf16), lam[:, 3:].astype(bf16))
    matrix = tap_matrix(weight)
    flipped = tap_matrix(weight[::-1].transpose(0, 2, 1))
    offset = jnp.broadcast_to(jnp.tile(bias, 2)[:, None], (128, 256))
    diagonal = jnp.diagonal(weight[13]).astype(f32)
    diag = jnp.broadcast_to((2.0 * STEP * diagonal)[:, None], (64, 128))
    ones = jnp.ones((4,), f32)
    mask = jnp.concatenate([(slab > 0).astype(f32)[None], ones, (slab < slabs - 1).astype(f32)[None]])
    cot1, sens, state, start, factor = forward(mask, u, u_lo, u_hi, lam, matrix, offset, diag)
    cot_lo, cot_hi = neighbours(cot1[:2], cot1[2:])
    factors = exchanged(factor.reshape(8, 2, 64, 128), "tm")
    scale = STEP / math.sqrt(2 * devices * 4 * 8 * 256)
    partial_sum = gradient(scale, cot1, state)
    cot0, coarse, average_lam = backward(mask, cot1, cot_lo, cot_hi, lam, lam_lo, lam_hi, sens, flipped, factor)
    pieces = exchanged(coarse.reshape(8, 2, 64, 128), "tm")
    total = gradient(scale, cot0, start, partial_sum)
    parts = exchanged(total.reshape(devices, 8, 128), ("tm", "slab"))
    carried = exchanged(sweep(factors, pieces), "tm").reshape(4, 4, 64, 128)
    mine = jnp.sum(parts, axis=0)
    summed = exchanged(jnp.broadcast_to(mine[None], parts.shape), ("tm", "slab")).reshape(16, 64, 128)
    updated = finish(lam, average_lam, carried)
    return updated[None], taps_of(summed), jnp.sum(summed[14], axis=1)


def solution(mesh):
    in_specs = (P("tm", None, "slab", None, None), P("tm", None, "slab", None, None), P(), P())
    out_specs = (P("tm", None, "slab", None, None), P(), P())
    return jax.shard_map(
        on_device, mesh=mesh, in_specs=in_specs, out_specs=out_specs, check_vma=False
    )
```

```python
import functools
import math

import jax
import jax.numpy as jnp
from jax import lax
from jax.experimental import pallas as pl
from jax.experimental.pallas import tpu as pltpu
from jax.sharding import PartitionSpec as P

f32, bf16 = jnp.float32, jnp.bfloat16
STEP = 0.25


def shifts(value):
    lane = lax.broadcasted_iota(jnp.int32, value.shape, 1)
    zero = jnp.zeros((), value.dtype)
    left = jnp.where(lane == 0, zero, pltpu.roll(value, 1, 1))
    right = jnp.where(lane == 255, zero, pltpu.roll(value, 255, 1))
    return left, right


def put(wide, plane, row, pair, value):
    count = value.shape[0]
    left, right = shifts(value)
    base = plane * 384 + row
    cols = slice(pair * 256, pair * 256 + 256)
    wide[pl.ds(base, count), cols] = left
    wide[pl.ds(base + 128, count), cols] = value
    wide[pl.ds(base + 256, count), cols] = right


def to_rows(source, z, turn):
    value = source[:, z].astype(f32).reshape(512, 256)
    turn[0] = value[:, :128]
    turn[1] = value[:, 128:]


def row_of(turn, x):
    return jnp.concatenate([turn[half, pl.ds(x, 64, stride=8), :] for half in range(2)], 1)


def pair_of(turn, pair):
    return jnp.concatenate([row_of(turn, 2 * pair), row_of(turn, 2 * pair + 1)], 0)


def products(matrix, wide, z):
    base = pl.multiple_of(z * 384, 384)
    return [
        jnp.dot(
            matrix[...],
            wide[pl.ds(base, 1152), pair * 256 : pair * 256 + 256],
            preferred_element_type=f32,
        )
        for pair in range(4)
    ]


def combined(parts, pair):
    low, high = parts[pair][0:64], parts[pair][64:128]
    if pair > 0:
        low = low + parts[pair - 1][192:256]
    if pair < 3:
        high = high + parts[pair + 1][128:192]
    return jnp.concatenate([low, high], 0)


def averaging():
    fine = lax.broadcasted_iota(jnp.int32, (256, 128), 0)
    coarse = lax.broadcasted_iota(jnp.int32, (256, 128), 1)
    return jnp.where((fine == 2 * coarse) | (fine == 2 * coarse + 1), 0.25, 0.0).astype(bf16)


def split_dot(value, matrix):
    high = value.astype(bf16)
    low = (value - high.astype(f32)).astype(bf16)
    return jnp.dot(high, matrix, preferred_element_type=f32) + jnp.dot(
        low, matrix, preferred_element_type=f32
    )


def field(planes, dtype):
    return pltpu.VMEM((planes, 128, 1024), dtype)


def widened(planes):
    return pltpu.VMEM((planes * 384, 1024), bf16)


def near(value):
    return pltpu.with_memory_space_constraint(value, pltpu.VMEM)


def run(body, name, micros, outs, ins, scratch=(), aliases=None, scalars=0, limit=8):
    in_specs = [pl.BlockSpec(memory_space=pltpu.SMEM)] * scalars
    in_specs += [pl.BlockSpec(memory_space=pltpu.VMEM)] * (len(ins) - scalars)
    return pl.pallas_call(
        body,
        out_shape=outs,
        in_specs=in_specs,
        scratch_shapes=list(scratch),
        input_output_aliases=aliases or {},
        compiler_params=pltpu.CompilerParams(vmem_limit_bytes=limit * 2**20),
        cost_estimate=pl.CostEstimate(flops=int(micros * 1.1e9), bytes_accessed=0, transcendentals=0),
        name=name,
    )(*ins)


TURN = pltpu.VMEM((2, 512, 128), f32)


def open_body(u, low, high, turn):
    for z in range(4):
        to_rows(u, z, turn)
        target = low if z < 2 else high
        for pair in range(4):
            target[z % 2, :, pair * 256 : pair * 256 + 256] = pair_of(turn, pair).astype(bf16)


def step_state(z, matrix, offset, wide0, wide1, sens, weight):
    parts = products(matrix, wide0, z)
    base = pl.multiple_of((z + 1) * 384, 384)
    for pair in range(4):
        cols = slice(pair * 256, pair * 256 + 256)
        tanh = jnp.tanh(combined(parts, pair) + offset)
        sens[z, :, cols] = 1.0 - tanh * tanh
        value = wide0[pl.ds(base + 128, 128), cols].astype(f32) + STEP * tanh
        if weight is not None:
            value = value * weight
        put(wide1, z, 0, pair, value.astype(bf16))


def inner_body(low, high, lam, matrix, bias, wide0, wide1, sens, lam_rows, average_lam, turn):
    average = averaging()
    for z in range(4):
        source = low if z < 2 else high
        for pair in range(4):
            put(wide0, z + 2, 0, pair, source[z % 2, :, pair * 256 : pair * 256 + 256])
    offset = bias[...]

    def inside(z, carry):
        step_state(z, matrix, offset, wide0, wide1, sens, None)
        return carry

    lax.fori_loop(2, 4, inside, 0)
    for z in range(4):
        to_rows(lam, z, turn)
        for pair in range(4):
            cols = slice(pair * 256, pair * 256 + 256)
            value = pair_of(turn, pair)
            lam_rows[z, :, cols] = value
            average_lam[z, pair] = split_dot(value[0:64] + value[64:128], average)


def forward_body(mask, wide0_in, wide1_in, sens_in, u_lo, u_hi, lam, matrix, bias, diag, wide0, wide1, sens, cot_low, cot_high, factor):
    for z in range(2):
        for pair in range(4):
            cols = slice(pair * 256, pair * 256 + 256)
            put(wide0, z, 0, pair, u_lo[z, :, cols])
            put(wide0, z + 6, 0, pair, u_hi[z, :, cols])
    offset = bias[...]

    def outside(index, carry):
        z = index + 2 * (index // 2)
        step_state(z, matrix, offset, wide0, wide1, sens, mask[z])
        return carry

    lax.fori_loop(0, 4, outside, 0)
    average = averaging()

    def second(z, target, place):
        parts = products(matrix, wide1, z)
        for pair in range(4):
            cols = slice(pair * 256, pair * 256 + 256)
            tanh = jnp.tanh(combined(parts, pair) + offset)
            target[place, :, cols] = ((1.0 - tanh * tanh) * lam[z, :, cols]).astype(bf16)
            both = sens[z + 1, 0:64, cols] + sens[z + 1, 64:128, cols]
            coarse = jnp.dot(both.astype(bf16), average, preferred_element_type=f32)
            factor[z, pair] = (coarse * diag[...]).astype(bf16)

    def second_low(z, carry):
        second(z, cot_low, z)
        return carry

    def second_high(z, carry):
        second(z + 2, cot_high, z)
        return carry

    cot_low[2] = lam[0].astype(bf16)
    cot_high[2] = lam[3].astype(bf16)
    lax.fori_loop(0, 2, second_low, 0)
    lax.fori_loop(0, 2, second_high, 0)


def step_back(z, matrix, wide1, wide0, middle, sens, lam, weight):
    parts = products(matrix, wide1, z)
    for pair in range(4):
        cols = slice(pair * 256, pair * 256 + 256)
        value = lam(cols) + STEP * combined(parts, pair)
        middle[z, :, cols] = value
        value = sens[z, :, cols] * value
        if weight is not None:
            value = value * weight
        put(wide0, z, 0, pair, value.astype(bf16))


def back_inner_body(low, high, lam, sens, matrix, wide1, wide0, middle):
    for z in range(4):
        source = low if z < 2 else high
        for pair in range(4):
            put(wide1, z + 2, 0, pair, source[z % 2, :, pair * 256 : pair * 256 + 256])

    def inside(z, carry):
        step_back(z, matrix, wide1, wide0, middle, sens, lambda cols: lam[z - 1, :, cols], None)
        return carry

    lax.fori_loop(2, 4, inside, 0)


def back_outer_body(mask, wide1_in, wide0_in, middle_in, cot_lo, cot_hi, lam, sens, matrix, wide1, wide0, middle):
    for z in range(2):
        for pair in range(4):
            cols = slice(pair * 256, pair * 256 + 256)
            put(wide1, z, 0, pair, cot_lo[z, :, cols])
            put(wide1, z + 6, 0, pair, cot_hi[z, :, cols])

    def outside(index, carry):
        z = 1 + 3 * index
        step_back(z, matrix, wide1, wide0, middle, sens, lambda cols: lam[z - 1, :, cols], None)
        return carry

    step_back(0, matrix, wide1, wide0, middle, sens, lambda cols: cot_lo[2, :, cols].astype(f32), mask[0])
    lax.fori_loop(0, 2, outside, 0)
    step_back(5, matrix, wide1, wide0, middle, sens, lambda cols: cot_hi[2, :, cols].astype(f32), mask[5])


def back_last_body(wide0, middle, average_lam, factor, matrix, coarse, kept):
    average = averaging()

    def last(z, carry):
        parts = products(matrix, wide0, z)
        for pair in range(4):
            cols = slice(pair * 256, pair * 256 + 256)
            value = middle[z + 1, :, cols] + STEP * combined(parts, pair)
            back = split_dot(value[0:64] + value[64:128], average)
            here = average_lam[z, pair]
            kept[z, pair] = here
            coarse[z, pair] = (back - here - factor[z, pair].astype(f32) * here).astype(bf16)
        return carry

    lax.fori_loop(0, 4, last, 0)


def gradient_body(scale, count, first, *refs):
    cots, wide, rest = refs[:count], refs[count], refs[count + 1 :]
    earlier, coarse, factor = rest[:3] if len(rest) == 6 else (None, None, None)
    out, widened_cot, total = rest[-3:]
    sums = jnp.zeros((128, 128), f32)
    zero = jnp.zeros((64, 256), bf16)
    for z in range(4):
        if count == 2:
            value = cots[z // 2][z % 2]
        else:
            value = cots[0][(z + 1) * 384 + 128 : (z + 1) * 384 + 256, :]
        widened_cot[z, 0:128] = value
        widened_cot[z, 128:192] = jnp.concatenate([zero, value[64:128, :768]], 1)
        widened_cot[z, 192:256] = jnp.concatenate([value[0:64, 256:], zero], 1)
        for part in range(8):
            sums = sums + value[:, part * 128 : part * 128 + 128].astype(f32)
    total[...] = jnp.zeros_like(total)

    def plane(z, carry):
        base = pl.multiple_of((z + first) * 384, 384)
        total[...] += lax.dot_general(
            widened_cot[z],
            wide[pl.ds(base, 1152), :],
            (((1,), (1,)), ((), ())),
            preferred_element_type=f32,
        )
        return carry

    lax.fori_loop(0, 4, plane, 0)
    lower = lax.broadcasted_iota(jnp.int32, (64, 128), 1) < 64

    def give(block, value):
        if earlier is None:
            out[block] = value
        else:
            start = 256 + 64 * (block % 2)
            out[block // 2, start : start + 64] = ((value + earlier[block]) * scale).astype(bf16)

    for tap in range(9):
        cols = slice(tap * 128, tap * 128 + 128)
        rows = [total[64 * q : 64 * q + 64, cols] for q in range(4)]
        taps = [jnp.where(lower, rows[1], rows[3]), jnp.where(lower, rows[0], rows[1]), jnp.where(lower, rows[2], rows[0])]
        taps = [value + pltpu.roll(value, 64, 1) for value in taps]
        give(tap, jnp.where(lower, taps[0], taps[1]))
        if tap % 2 == 0:
            kept = taps[2]
        else:
            give(9 + tap // 2, jnp.where(lower, kept, taps[2]))
    give(13, kept)
    give(14, sums[0:64] + sums[64:128])
    give(15, jnp.zeros((64, 128), f32))
    if earlier is not None:
        for group in range(8):
            out[group, 0:128] = coarse[group]
            out[group, 128:256] = factor[group]


def gradient(scale, cots, wide, first, *extra):
    ins = [near(value) for value in (*cots, wide, *extra)]
    return run(
        functools.partial(gradient_body, scale, len(cots), first),
        "gradient",
        5,
        jax.ShapeDtypeStruct((8, 384, 128), bf16) if extra else pltpu.VMEM((16, 64, 128), f32),
        ins,
        [pltpu.VMEM((4, 256, 1024), bf16), pltpu.VMEM((256, 1152), f32)],
    )


def meet_body(mixed, out, shared):
    groups = mixed.shape[0]
    value = jnp.zeros((128, 128), f32)
    out[0] = value.astype(bf16)
    summed = mixed[0, 256:384].astype(f32)
    for group in range(groups - 1):
        value = value + mixed[group, 128:256].astype(f32) * value + mixed[group, 0:128].astype(f32)
        out[group + 1] = value.astype(bf16)
        summed = summed + mixed[group + 1, 256:384].astype(f32)
    summed = summed.astype(bf16)
    for slab in range(shared.shape[0]):
        shared[slab] = summed


def join_body(shared, carried, out):
    summed = shared[0].astype(f32)
    for slab in range(1, shared.shape[0]):
        summed = summed + shared[slab].astype(f32)
    summed = summed.astype(bf16)
    for group in range(out.shape[0]):
        out[group, 0:128] = carried[group]
        out[group, 128:256] = summed


def finish_body(lam, average_lam, joined, out, taps, offset, turn):
    fine = lax.broadcasted_iota(jnp.int32, (128, 256), 1)
    coarse = lax.broadcasted_iota(jnp.int32, (128, 256), 0)
    copies = jnp.where((fine == 2 * coarse) | (fine == 2 * coarse + 1), 1.0, 0.0).astype(bf16)

    def plane(z, carry):
        for pair in range(4):
            carried = joined[2 * z + pair // 2, 64 * (pair % 2) : 64 * (pair % 2) + 64]
            value = split_dot(carried.astype(f32) - average_lam[z, pair], copies)
            for half in range(2):
                for x in (2 * pair, 2 * pair + 1):
                    turn[half, pl.ds(x, 64, stride=8), :] = value[:, half * 128 : half * 128 + 128]
        added = jnp.concatenate([turn[0], turn[1]], 1).reshape(64, 8, 256)
        out[:, z] = lam[:, z] + added
        return carry

    lax.fori_loop(0, 4, plane, 0)

    def block(index):
        start = 128 + 64 * (index % 2)
        return joined[index // 2, start : start + 64].astype(f32)

    for a in range(3):
        for c in range(3):
            tap = 3 * a + c
            both = block(tap)
            taps[9 * a + c] = both[:, :64]
            taps[9 * a + 3 + c] = both[:, 64:]
            half = 64 * (tap % 2)
            taps[9 * a + 6 + c] = block(9 + tap // 2)[:, half : half + 64]
    row = lax.broadcasted_iota(jnp.int32, (64, 64), 0)
    col = lax.broadcasted_iota(jnp.int32, (64, 64), 1)
    column = jnp.broadcast_to(jnp.sum(block(14), axis=1, keepdims=True), (64, 64))
    offset[...] = jnp.sum(jnp.where(row == col, column, 0.0), axis=0, keepdims=True)


def prepare_body(mask, weight, bias, matrix, flipped, offset, diag):
    row = lax.broadcasted_iota(jnp.int32, (64, 64), 0)
    col = lax.broadcasted_iota(jnp.int32, (64, 64), 1)
    zero = jnp.zeros((64, 64), f32)

    def column(values):
        return jnp.sum(jnp.where(row == col, values, 0.0), axis=1, keepdims=True)

    def build(out, tap):
        for a in range(3):
            for c in range(3):
                taps = [tap(9 * a + 3 * b + c) for b in range(3)]
                sides = ((taps[1], taps[2]), (taps[0], taps[1]), (taps[2], zero), (zero, taps[0]))
                start = (3 * a + c) * 128
                for place in range(4):
                    both = jnp.concatenate(sides[place], 1)
                    out[64 * place : 64 * place + 64, start : start + 128] = both.astype(bf16)

    build(matrix, lambda tap: weight[tap].astype(f32))
    build(flipped, lambda tap: weight[26 - tap].astype(f32).T)
    column_bias = jnp.broadcast_to(column(jnp.broadcast_to(bias[...], (64, 64))), (64, 256))
    offset[0:64] = column_bias
    offset[64:128] = column_bias
    diag[...] = jnp.broadcast_to(2.0 * STEP * column(weight[13].astype(f32)), (64, 128))


def neighbours(low_part, high_part):
    count = lax.axis_size("slab")
    up = [(i, i + 1) for i in range(count - 1)]
    down = [(i + 1, i) for i in range(count - 1)]
    return lax.ppermute(high_part, "slab", up), lax.ppermute(low_part, "slab", down)


def exchanged(value, axes):
    return lax.all_to_all(value, axes, 0, 0, tiled=True)


def on_device(u_states, lam_points, weight, bias):
    u, lam = u_states[0], lam_points[0]
    slab, slabs = lax.axis_index("slab"), lax.axis_size("slab")
    groups = lax.axis_size("tm")
    half = field(2, bf16)
    ones = jnp.ones((4,), f32)
    mask = jnp.concatenate([(slab > 0).astype(f32)[None], ones, (slab < slabs - 1).astype(f32)[None]])
    u_low, u_high = run(open_body, "open", 3, (half, half), [u], [TURN])
    u_lo, u_hi = neighbours(u_low, u_high)
    taps = pltpu.VMEM((256, 1152), bf16)
    matrix, flipped, offset, diag = run(
        prepare_body,
        "prepare",
        2,
        (taps, taps, pltpu.VMEM((128, 256), f32), pltpu.VMEM((64, 128), f32)),
        [mask, weight, bias[None]],
        scalars=1,
    )
    matrix, flipped, offset, diag = (near(v) for v in (matrix, flipped, offset, diag))
    coarse_shape = pltpu.VMEM((4, 4, 64, 128), bf16)
    average_shape = (4, 4, 64, 128)
    wide0, wide1, sens, lam_rows, average_lam = run(
        inner_body,
        "inner",
        5,
        (
            widened(8),
            widened(6),
            field(6, f32),
            field(4, f32),
            pltpu.VMEM(average_shape, f32),
        ),
        [near(u_low), near(u_high), lam, matrix, offset],
        [TURN],
    )
    wide0, wide1, sens, cot_low, cot_high, factor = run(
        forward_body,
        "forward",
        10,
        (widened(8), widened(6), field(6, f32), field(3, bf16), field(3, bf16), coarse_shape),
        [mask]
        + [near(v) for v in (wide0, wide1, sens, u_lo, u_hi, lam_rows)]
        + [matrix, offset, diag],
        aliases={1: 0, 2: 1, 3: 2},
        scalars=1,
    )
    cot_lo, cot_hi = neighbours(cot_low, cot_high)
    scale = STEP / math.sqrt(2 * groups * slabs * 4 * 8 * 256)
    earlier = gradient(scale, (cot_low, cot_high), wide1, 0)
    back1, back0, middle = run(
        back_inner_body,
        "back_inner",
        3,
        (widened(8), widened(6), field(6, f32)),
        [near(v) for v in (cot_low, cot_high, lam_rows, sens)] + [flipped],
    )
    back1, back0, middle = run(
        back_outer_body,
        "back_outer",
        5,
        (widened(8), widened(6), field(6, f32)),
        [mask]
        + [near(v) for v in (back1, back0, middle, cot_lo, cot_hi, lam_rows, sens)]
        + [flipped],
        aliases={1: 0, 2: 1, 3: 2},
        scalars=1,
    )
    coarse, average_lam = run(
        back_last_body,
        "back_last",
        5,
        (coarse_shape, jax.ShapeDtypeStruct(average_shape, f32)),
        [near(v) for v in (back0, middle, average_lam, factor)] + [flipped],
    )
    pieces = (groups, 128, 128)
    mixed = gradient(scale, (back0,), wide0, 1, earlier, coarse.reshape(pieces), factor.reshape(pieces))
    carried, shared = run(
        meet_body,
        "meet",
        1,
        (jax.ShapeDtypeStruct(pieces, bf16), jax.ShapeDtypeStruct((slabs, 128, 128), bf16)),
        [exchanged(mixed, "tm")],
    )
    joined = run(
        join_body,
        "join",
        1,
        jax.ShapeDtypeStruct((groups, 256, 128), bf16),
        [exchanged(shared, "slab"), carried],
    )
    updated, taps, offset = run(
        finish_body,
        "finish",
        4,
        (
            jax.ShapeDtypeStruct(lam.shape, f32),
            jax.ShapeDtypeStruct(weight.shape, f32),
            jax.ShapeDtypeStruct((1, 64), f32),
        ),
        [lam, average_lam, exchanged(joined, "tm")],
        [TURN],
    )
    return updated[None], taps, offset[0]


def solution(mesh):
    in_specs = (P("tm", None, "slab", None, None), P("tm", None, "slab", None, None), P(), P())
    out_specs = (P("tm", None, "slab", None, None), P(), P())
    return jax.shard_map(
        on_device, mesh=mesh, in_specs=in_specs, out_specs=out_specs, check_vma=False
    )
```

```python
import functools
import math

import jax
import jax.numpy as jnp
from jax import lax
from jax.experimental import pallas as pl
from jax.experimental.pallas import tpu as pltpu
from jax.sharding import PartitionSpec as P

f32, bf16 = jnp.float32, jnp.bfloat16
STEP = 0.25


def shifts(value):
    lane = lax.broadcasted_iota(jnp.int32, value.shape, 1)
    zero = jnp.zeros((), value.dtype)
    left = jnp.where(lane == 0, zero, pltpu.roll(value, 1, 1))
    right = jnp.where(lane == 255, zero, pltpu.roll(value, 255, 1))
    return left, right


def put(wide, plane, row, pair, value):
    count = value.shape[0]
    left, right = shifts(value)
    base = pl.multiple_of(plane * 384 + row, 64)
    cols = slice(pair * 256, pair * 256 + 256)
    wide[pl.ds(base, count), cols] = left
    wide[pl.ds(base + 128, count), cols] = value
    wide[pl.ds(base + 256, count), cols] = right


def to_rows(source, z, turn):
    value = source[:, z].astype(f32).reshape(512, 256)
    turn[0] = value[:, :128]
    turn[1] = value[:, 128:]


def row_of(turn, x):
    return jnp.concatenate([turn[half, pl.ds(x, 64, stride=8), :] for half in range(2)], 1)


def pair_of(turn, pair):
    return jnp.concatenate([row_of(turn, 2 * pair), row_of(turn, 2 * pair + 1)], 0)


def products(matrix, wide, z):
    base = pl.multiple_of(z * 384, 384)
    return [
        jnp.dot(
            matrix[...],
            wide[pl.ds(base, 1152), pair * 256 : pair * 256 + 256],
            preferred_element_type=f32,
        )
        for pair in range(4)
    ]


def combined(parts, pair):
    low, high = parts[pair][0:64], parts[pair][64:128]
    if pair > 0:
        low = low + parts[pair - 1][192:256]
    if pair < 3:
        high = high + parts[pair + 1][128:192]
    return jnp.concatenate([low, high], 0)


def averaging():
    fine = lax.broadcasted_iota(jnp.int32, (256, 128), 0)
    coarse = lax.broadcasted_iota(jnp.int32, (256, 128), 1)
    return jnp.where((fine == 2 * coarse) | (fine == 2 * coarse + 1), 0.25, 0.0).astype(bf16)


def split_dot(value, matrix):
    high = value.astype(bf16)
    low = (value - high.astype(f32)).astype(bf16)
    return jnp.dot(high, matrix, preferred_element_type=f32) + jnp.dot(
        low, matrix, preferred_element_type=f32
    )


def field(planes, dtype):
    return pltpu.VMEM((planes, 128, 1024), dtype)


def widened(planes):
    return pltpu.VMEM((planes * 384, 1024), bf16)


def near(value):
    return pltpu.with_memory_space_constraint(value, pltpu.VMEM)


def run(body, name, micros, outs, ins, scratch=(), aliases=None, scalars=0, limit=8):
    in_specs = [pl.BlockSpec(memory_space=pltpu.SMEM)] * scalars
    in_specs += [pl.BlockSpec(memory_space=pltpu.VMEM)] * (len(ins) - scalars)
    return pl.pallas_call(
        body,
        out_shape=outs,
        in_specs=in_specs,
        scratch_shapes=list(scratch),
        input_output_aliases=aliases or {},
        compiler_params=pltpu.CompilerParams(vmem_limit_bytes=limit * 2**20),
        cost_estimate=pl.CostEstimate(flops=int(micros * 1.1e9), bytes_accessed=0, transcendentals=0),
        name=name,
    )(*ins)


TURN = pltpu.VMEM((2, 512, 128), f32)


def sides(spot):
    odd = spot[0]
    return 2 * (1 - odd), 2 * odd


def open_body(spot, u, out_a, out_b, turn):
    for base, target in zip(sides(spot), (out_a, out_b)):
        for place in range(2):
            to_rows(u, base + place, turn)
            for pair in range(4):
                target[place, :, pair * 256 : pair * 256 + 256] = pair_of(turn, pair).astype(bf16)


def put_planes(wide, z, source):
    for place in range(2):
        for pair in range(4):
            put(wide, z + place, 0, pair, source[place, :, pair * 256 : pair * 256 + 256])


def step_state(z, matrix, offset, wide0, wide1, sens, weight):
    parts = products(matrix, wide0, z)
    base = pl.multiple_of((z + 1) * 384, 384)
    for pair in range(4):
        cols = slice(pair * 256, pair * 256 + 256)
        tanh = jnp.tanh(combined(parts, pair) + offset)
        sens[z, :, cols] = 1.0 - tanh * tanh
        value = wide0[pl.ds(base + 128, 128), cols].astype(f32) + STEP * tanh
        if weight is not None:
            value = value * weight
        put(wide1, z, 0, pair, value.astype(bf16))


def inner_body(spot, own_a, own_b, lam, matrix, bias, wide0, wide1, sens, lam_rows, average_lam, turn):
    average = averaging()
    for base, source in zip(sides(spot), (own_a, own_b)):
        put_planes(wide0, base + 2, source)
    offset = bias[...]

    def inside(z, carry):
        step_state(z, matrix, offset, wide0, wide1, sens, None)
        return carry

    lax.fori_loop(2, 4, inside, 0)
    for z in range(4):
        to_rows(lam, z, turn)
        for pair in range(4):
            cols = slice(pair * 256, pair * 256 + 256)
            value = pair_of(turn, pair)
            lam_rows[z, :, cols] = value
            average_lam[z, pair] = split_dot(value[0:64] + value[64:128], average)


def forward_body(spot, mask, wide0_in, wide1_in, sens_in, u_a, u_b, lam, matrix, bias, diag, wide0, wide1, sens, cot_a, cot_b, factor):
    for base, source in zip(sides(spot), (u_a, u_b)):
        put_planes(wide0, 3 * base, source)
    offset = bias[...]

    def outside(index, carry):
        z = index + 2 * (index // 2)
        step_state(z, matrix, offset, wide0, wide1, sens, mask[z])
        return carry

    lax.fori_loop(0, 4, outside, 0)
    average = averaging()

    def second(z, target, place):
        parts = products(matrix, wide1, z)
        for pair in range(4):
            cols = slice(pair * 256, pair * 256 + 256)
            tanh = jnp.tanh(combined(parts, pair) + offset)
            target[place, :, cols] = ((1.0 - tanh * tanh) * lam[z, :, cols]).astype(bf16)
            both = sens[z + 1, 0:64, cols] + sens[z + 1, 64:128, cols]
            coarse = jnp.dot(both.astype(bf16), average, preferred_element_type=f32)
            factor[z, pair] = (coarse * diag[...]).astype(bf16)

    for base, target in zip(sides(spot), (cot_a, cot_b)):
        target[2] = lam[base + base // 2].astype(bf16)

        def plane(place, carry, base=base, target=target):
            second(base + place, target, place)
            return carry

        lax.fori_loop(0, 2, plane, 0)


def step_back(z, matrix, wide1, wide0, middle, sens, lam, weight):
    parts = products(matrix, wide1, z)
    for pair in range(4):
        cols = slice(pair * 256, pair * 256 + 256)
        value = lam(cols) + STEP * combined(parts, pair)
        middle[z, :, cols] = value
        value = sens[z, :, cols] * value
        if weight is not None:
            value = value * weight
        put(wide0, z, 0, pair, value.astype(bf16))


def back_inner_body(spot, own_a, own_b, lam, sens, matrix, wide1, wide0, middle):
    for base, source in zip(sides(spot), (own_a, own_b)):
        put_planes(wide1, base + 2, source)

    def inside(z, carry):
        step_back(z, matrix, wide1, wide0, middle, sens, lambda cols: lam[z - 1, :, cols], None)
        return carry

    lax.fori_loop(2, 4, inside, 0)


def back_outer_body(spot, mask, wide1_in, wide0_in, middle_in, cot_a, cot_b, lam, sens, matrix, wide1, wide0, middle):
    for base, source in zip(sides(spot), (cot_a, cot_b)):
        put_planes(wide1, 3 * base, source)

    def outside(index, carry):
        z = 1 + 3 * index
        step_back(z, matrix, wide1, wide0, middle, sens, lambda cols: lam[z - 1, :, cols], None)
        return carry

    lax.fori_loop(0, 2, outside, 0)
    for base, source in zip(sides(spot), (cot_a, cot_b)):
        z = 2 * base + base // 2
        step_back(z, matrix, wide1, wide0, middle, sens, lambda cols: source[2, :, cols].astype(f32), mask[z])


def back_last_body(wide0, middle, average_lam, factor, matrix, coarse, kept):
    average = averaging()

    def last(z, carry):
        parts = products(matrix, wide0, z)
        for pair in range(4):
            cols = slice(pair * 256, pair * 256 + 256)
            value = middle[z + 1, :, cols] + STEP * combined(parts, pair)
            back = split_dot(value[0:64] + value[64:128], average)
            here = average_lam[z, pair]
            kept[z, pair] = here
            coarse[z, pair] = (back - here - factor[z, pair].astype(f32) * here).astype(bf16)
        return carry

    lax.fori_loop(0, 4, last, 0)


def gradient_body(scale, spot, *refs):
    last = len(refs) == 8
    cots, wide, rest = (refs[:1], refs[1], refs[2:]) if last else (refs[:2], refs[2], refs[3:])
    if last:
        earlier, mine, others, out, widened_cot, total = rest
    else:
        out, widened_cot, total = rest
    sums = jnp.zeros((128, 128), f32)
    zero = jnp.zeros((64, 256), bf16)
    side_a, side_b = sides(spot)
    for z in range(4):
        if last:
            value = cots[0][(z + 1) * 384 + 128 : (z + 1) * 384 + 256, :]
        else:
            value = cots[z // 2][z % 2]
        widened_cot[z, 0:128] = value
        widened_cot[z, 128:192] = jnp.concatenate([zero, value[64:128, :768]], 1)
        widened_cot[z, 192:256] = jnp.concatenate([value[0:64, 256:], zero], 1)
        for part in range(8):
            sums = sums + value[:, part * 128 : part * 128 + 128].astype(f32)
    total[...] = jnp.zeros_like(total)

    def plane(z, carry):
        above = z + 1 if last else jnp.where(z < 2, side_a, side_b) + z % 2
        base = pl.multiple_of(above * 384, 384)
        total[...] += lax.dot_general(
            widened_cot[z],
            wide[pl.ds(base, 1152), :],
            (((1,), (1,)), ((), ())),
            preferred_element_type=f32,
        )
        return carry

    lax.fori_loop(0, 4, plane, 0)
    lower = lax.broadcasted_iota(jnp.int32, (64, 128), 1) < 64

    def give(block, value):
        out[block] = (value + earlier[block]) * scale if last else value

    for tap in range(9):
        cols = slice(tap * 128, tap * 128 + 128)
        rows = [total[64 * q : 64 * q + 64, cols] for q in range(4)]
        taps = [jnp.where(lower, rows[1], rows[3]), jnp.where(lower, rows[0], rows[1]), jnp.where(lower, rows[2], rows[0])]
        taps = [value + pltpu.roll(value, 64, 1) for value in taps]
        give(tap, jnp.where(lower, taps[0], taps[1]))
        if tap % 2 == 0:
            kept = taps[2]
        else:
            give(9 + tap // 2, jnp.where(lower, kept, taps[2]))
    give(13, kept)
    give(14, sums[0:64] + sums[64:128])
    give(15, jnp.zeros((64, 128), f32))
    if last:
        for block in range(8):
            mine[block] = out[block + 8 * spot[0]]
            others[block] = out[block + 8 - 8 * spot[0]]


def gradient(scale, spot, cots, wide, earlier=None):
    blocks, half = pltpu.VMEM((16, 64, 128), f32), pltpu.VMEM((8, 64, 128), f32)
    ins = [*cots, wide] if earlier is None else [*cots, wide, earlier]
    return run(
        functools.partial(gradient_body, scale),
        "gradient",
        5,
        blocks if earlier is None else (half, half),
        [spot] + [near(value) for value in ins],
        ([] if earlier is None else [blocks]) + [pltpu.VMEM((4, 256, 1024), bf16), pltpu.VMEM((256, 1152), f32)],
        scalars=1,
    )


def pack_body(mine, received, coarse, factor, out):
    for group in range(out.shape[0]):
        out[group, 0:128] = coarse[group]
        out[group, 128:256] = factor[group]
        out[group, 256:320] = (mine[group] + received[group]).astype(bf16)


def meet_body(mixed, out, shared):
    groups = mixed.shape[0]
    value = jnp.zeros((128, 128), f32)
    out[0] = value.astype(bf16)
    summed = mixed[0, 256:320].astype(f32)
    for group in range(groups - 1):
        value = value + mixed[group, 128:256].astype(f32) * value + mixed[group, 0:128].astype(f32)
        out[group + 1] = value.astype(bf16)
        summed = summed + mixed[group + 1, 256:320].astype(f32)
    summed = summed.astype(bf16)
    for chip in range(shared.shape[0]):
        shared[chip] = summed


def join_body(shared, carried, out):
    summed = shared[0].astype(f32)
    for chip in range(1, shared.shape[0]):
        summed = summed + shared[chip].astype(f32)
    summed = summed.astype(bf16)
    for group in range(out.shape[0]):
        out[group, 0:128] = carried[group]
        out[group, 128:192] = summed


def finish_body(lam, average_lam, joined, out, turn):
    fine = lax.broadcasted_iota(jnp.int32, (128, 256), 1)
    coarse = lax.broadcasted_iota(jnp.int32, (128, 256), 0)
    copies = jnp.where((fine == 2 * coarse) | (fine == 2 * coarse + 1), 1.0, 0.0).astype(bf16)

    def plane(z, carry):
        for pair in range(4):
            carried = joined[2 * z + pair // 2, 64 * (pair % 2) : 64 * (pair % 2) + 64]
            value = split_dot(carried.astype(f32) - average_lam[z, pair], copies)
            for half in range(2):
                for x in (2 * pair, 2 * pair + 1):
                    turn[half, pl.ds(x, 64, stride=8), :] = value[:, half * 128 : half * 128 + 128]
        added = jnp.concatenate([turn[0], turn[1]], 1).reshape(64, 8, 256)
        out[:, z] = lam[:, z] + added
        return carry

    lax.fori_loop(0, 4, plane, 0)


def taps_body(spot, joined, received, taps, offset):
    def block(index):
        own = joined[index % 8, 128:192].astype(f32)
        other = received[index % 8].astype(f32)
        return jnp.where(spot[0] == index // 8, own, other)

    for a in range(3):
        for c in range(3):
            tap = 3 * a + c
            both = block(tap)
            taps[9 * a + c] = both[:, :64]
            taps[9 * a + 3 + c] = both[:, 64:]
            half = 64 * (tap % 2)
            taps[9 * a + 6 + c] = block(9 + tap // 2)[:, half : half + 64]
    row = lax.broadcasted_iota(jnp.int32, (64, 64), 0)
    col = lax.broadcasted_iota(jnp.int32, (64, 64), 1)
    column = jnp.broadcast_to(jnp.sum(block(14), axis=1, keepdims=True), (64, 64))
    offset[...] = jnp.sum(jnp.where(row == col, column, 0.0), axis=0, keepdims=True)


def prepare_body(mask, weight, bias, matrix, flipped, offset, diag):
    row = lax.broadcasted_iota(jnp.int32, (64, 64), 0)
    col = lax.broadcasted_iota(jnp.int32, (64, 64), 1)
    zero = jnp.zeros((64, 64), f32)

    def column(values):
        return jnp.sum(jnp.where(row == col, values, 0.0), axis=1, keepdims=True)

    def build(out, tap):
        for a in range(3):
            for c in range(3):
                taps = [tap(9 * a + 3 * b + c) for b in range(3)]
                sides = ((taps[1], taps[2]), (taps[0], taps[1]), (taps[2], zero), (zero, taps[0]))
                start = (3 * a + c) * 128
                for place in range(4):
                    both = jnp.concatenate(sides[place], 1)
                    out[64 * place : 64 * place + 64, start : start + 128] = both.astype(bf16)

    build(matrix, lambda tap: weight[tap].astype(f32))
    build(flipped, lambda tap: weight[26 - tap].astype(f32).T)
    column_bias = jnp.broadcast_to(column(jnp.broadcast_to(bias[...], (64, 64))), (64, 256))
    offset[0:64] = column_bias
    offset[64:128] = column_bias
    diag[...] = jnp.broadcast_to(2.0 * STEP * column(weight[13].astype(f32)), (64, 128))


def neighbours(side_a, side_b):
    count = lax.axis_size("slab")
    across = [(i, i + 1) for i in range(1, count - 1, 2)]
    from_b = lax.ppermute(side_b, "slab", across + [(j, i) for i, j in across])
    from_a = lax.ppermute(side_a, "slab", [(i, i ^ 1) for i in range(count)])
    return from_a, from_b


def exchanged(value, axes):
    return lax.all_to_all(value, axes, 0, 0, tiled=True)


def on_device(u_states, lam_points, weight, bias):
    u, lam = u_states[0], lam_points[0]
    slab, slabs = lax.axis_index("slab"), lax.axis_size("slab")
    groups = lax.axis_size("tm")
    half = field(2, bf16)
    ones = jnp.ones((4,), f32)
    mask = jnp.concatenate([(slab > 0).astype(f32)[None], ones, (slab < slabs - 1).astype(f32)[None]])
    spot = (slab % 2).astype(jnp.int32)[None]
    own_a, own_b = run(open_body, "open", 3, (half, half), [spot, u], [TURN], scalars=1)
    u_a, u_b = neighbours(own_a, own_b)
    taps = pltpu.VMEM((256, 1152), bf16)
    matrix, flipped, offset, diag = run(
        prepare_body,
        "prepare",
        2,
        (taps, taps, pltpu.VMEM((128, 256), f32), pltpu.VMEM((64, 128), f32)),
        [mask, weight, bias[None]],
        scalars=1,
    )
    matrix, flipped, offset, diag = (near(v) for v in (matrix, flipped, offset, diag))
    coarse_shape = pltpu.VMEM((4, 4, 64, 128), bf16)
    average_shape = (4, 4, 64, 128)
    wide0, wide1, sens, lam_rows, average_lam = run(
        inner_body,
        "inner",
        5,
        (
            widened(8),
            widened(6),
            field(6, f32),
            field(4, f32),
            pltpu.VMEM(average_shape, f32),
        ),
        [spot, near(own_a), near(own_b), lam, matrix, offset],
        [TURN],
        scalars=1,
    )
    wide0, wide1, sens, own_a, own_b, factor = run(
        forward_body,
        "forward",
        10,
        (widened(8), widened(6), field(6, f32), field(3, bf16), field(3, bf16), coarse_shape),
        [spot, mask]
        + [near(v) for v in (wide0, wide1, sens, u_a, u_b, lam_rows)]
        + [matrix, offset, diag],
        aliases={2: 0, 3: 1, 4: 2},
        scalars=2,
    )
    cot_a, cot_b = neighbours(own_a, own_b)
    scale = STEP / math.sqrt(2 * groups * slabs * 4 * 8 * 256)
    earlier = gradient(scale, spot, (own_a, own_b), wide1)
    back1, back0, middle = run(
        back_inner_body,
        "back_inner",
        3,
        (widened(8), widened(6), field(6, f32)),
        [spot] + [near(v) for v in (own_a, own_b, lam_rows, sens)] + [flipped],
        scalars=1,
    )
    back1, back0, middle = run(
        back_outer_body,
        "back_outer",
        5,
        (widened(8), widened(6), field(6, f32)),
        [spot, mask]
        + [near(v) for v in (back1, back0, middle, cot_a, cot_b, lam_rows, sens)]
        + [flipped],
        aliases={2: 0, 3: 1, 4: 2},
        scalars=2,
    )
    mine, others = gradient(scale, spot, (back0,), wide0, earlier)
    beside = [(i, i ^ 1) for i in range(slabs)]
    received = lax.ppermute(others, "slab", beside)
    coarse, average_lam = run(
        back_last_body,
        "back_last",
        5,
        (coarse_shape, jax.ShapeDtypeStruct(average_shape, f32)),
        [near(v) for v in (back0, middle, average_lam, factor)] + [flipped],
    )
    pieces = (groups, 128, 128)
    mixed = run(
        pack_body,
        "pack",
        1,
        jax.ShapeDtypeStruct((groups, 320, 128), bf16),
        [near(v) for v in (mine, received, coarse.reshape(pieces), factor.reshape(pieces))],
    )
    carried, shared = run(
        meet_body,
        "meet",
        1,
        (jax.ShapeDtypeStruct(pieces, bf16), jax.ShapeDtypeStruct((slabs // 2, 64, 128), bf16)),
        [exchanged(mixed, "tm")],
    )
    same_core = [list(range(core, slabs, 2)) for core in range(2)]
    shared = lax.all_to_all(shared, "slab", 0, 0, tiled=True, axis_index_groups=same_core)
    joined = run(
        join_body,
        "join",
        1,
        jax.ShapeDtypeStruct((groups, 192, 128), bf16),
        [shared, carried],
    )
    joined = exchanged(joined, "tm")
    received = lax.ppermute(joined[:, 128:], "slab", beside)
    updated = run(
        finish_body,
        "finish",
        3,
        jax.ShapeDtypeStruct(lam.shape, f32),
        [lam, average_lam, joined],
        [TURN],
    )
    taps, offset = run(
        taps_body,
        "taps",
        1,
        (jax.ShapeDtypeStruct(weight.shape, f32), jax.ShapeDtypeStruct((1, 64), f32)),
        [spot, joined, received],
        scalars=1,
    )
    return updated[None], taps, offset[0]


def solution(mesh):
    in_specs = (P("tm", None, "slab", None, None), P("tm", None, "slab", None, None), P(), P())
    out_specs = (P("tm", None, "slab", None, None), P(), P())
    return jax.shard_map(
        on_device, mesh=mesh, in_specs=in_specs, out_specs=out_specs, check_vma=False
    )
```

```python
import functools
import math

import jax
import jax.numpy as jnp
from jax import lax
from jax.experimental import pallas as pl
from jax.experimental.pallas import tpu as pltpu
from jax.sharding import PartitionSpec as P

f32, bf16 = jnp.float32, jnp.bfloat16
STEP = 0.25


def shifts(value):
    lane = lax.broadcasted_iota(jnp.int32, value.shape, 1)
    zero = jnp.zeros((), value.dtype)
    left = jnp.where(lane == 0, zero, pltpu.roll(value, 1, 1))
    right = jnp.where(lane == 255, zero, pltpu.roll(value, 255, 1))
    return left, right


def put(wide, plane, row, pair, value):
    count = value.shape[0]
    left, right = shifts(value)
    base = pl.multiple_of(plane * 384 + row, 64)
    cols = slice(pair * 256, pair * 256 + 256)
    wide[pl.ds(base, count), cols] = left
    wide[pl.ds(base + 128, count), cols] = value
    wide[pl.ds(base + 256, count), cols] = right


def to_rows(source, z, turn):
    value = source[:, z].astype(f32).reshape(512, 256)
    turn[0] = value[:, :128]
    turn[1] = value[:, 128:]


def row_of(turn, x):
    return jnp.concatenate([turn[half, pl.ds(x, 64, stride=8), :] for half in range(2)], 1)


def pair_of(turn, pair):
    return jnp.concatenate([row_of(turn, 2 * pair), row_of(turn, 2 * pair + 1)], 0)


def products(matrix, wide, z):
    base = pl.multiple_of(z * 384, 384)
    return [
        jnp.dot(
            matrix[...],
            wide[pl.ds(base, 1152), pair * 256 : pair * 256 + 256],
            preferred_element_type=f32,
        )
        for pair in range(4)
    ]


def combined(parts, pair):
    low, high = parts[pair][0:64], parts[pair][64:128]
    if pair > 0:
        low = low + parts[pair - 1][192:256]
    if pair < 3:
        high = high + parts[pair + 1][128:192]
    return jnp.concatenate([low, high], 0)


def averaging():
    fine = lax.broadcasted_iota(jnp.int32, (256, 128), 0)
    coarse = lax.broadcasted_iota(jnp.int32, (256, 128), 1)
    return jnp.where((fine == 2 * coarse) | (fine == 2 * coarse + 1), 0.25, 0.0).astype(bf16)


def split_dot(value, matrix):
    high = value.astype(bf16)
    low = (value - high.astype(f32)).astype(bf16)
    return jnp.dot(high, matrix, preferred_element_type=f32) + jnp.dot(
        low, matrix, preferred_element_type=f32
    )


def field(planes, dtype):
    return pltpu.VMEM((planes, 128, 1024), dtype)


def widened(planes):
    return pltpu.VMEM((planes * 384, 1024), bf16)


def near(value):
    return pltpu.with_memory_space_constraint(value, pltpu.VMEM)


def run(body, name, micros, outs, ins, scratch=(), aliases=None, scalars=0, limit=8):
    in_specs = [pl.BlockSpec(memory_space=pltpu.SMEM)] * scalars
    in_specs += [pl.BlockSpec(memory_space=pltpu.VMEM)] * (len(ins) - scalars)
    return pl.pallas_call(
        body,
        out_shape=outs,
        in_specs=in_specs,
        scratch_shapes=list(scratch),
        input_output_aliases=aliases or {},
        compiler_params=pltpu.CompilerParams(vmem_limit_bytes=limit * 2**20),
        cost_estimate=pl.CostEstimate(flops=int(micros * 1e8), bytes_accessed=0, transcendentals=0),
        name=name,
    )(*ins)


TURN = pltpu.VMEM((2, 512, 128), f32)


def sides(spot):
    odd = spot[0]
    return 2 * (1 - odd), 2 * odd


def open_body(side, spot, u, out, planes, turn, arrived):
    base = sides(spot)[side]
    copy = pltpu.make_async_copy(u.at[:, pl.ds(base, 2)], planes, arrived)
    copy.start()
    copy.wait()
    for place in range(2):
        to_rows(planes, place, turn)
        for pair in range(4):
            out[place, :, pair * 256 : pair * 256 + 256] = pair_of(turn, pair).astype(bf16)


def opened(side, spot, u):
    return pl.pallas_call(
        functools.partial(open_body, side),
        out_shape=field(2, bf16),
        in_specs=[pl.BlockSpec(memory_space=pltpu.SMEM), pl.BlockSpec(memory_space=pltpu.HBM)],
        scratch_shapes=[pltpu.VMEM((64, 2, 8, 256), bf16), TURN, pltpu.SemaphoreType.DMA(())],
        compiler_params=pltpu.CompilerParams(vmem_limit_bytes=8 * 2**20),
        cost_estimate=pl.CostEstimate(flops=10**8, bytes_accessed=0, transcendentals=0),
        name="open",
    )(spot, u)


def put_planes(wide, z, source):
    for place in range(2):
        for pair in range(4):
            put(wide, z + place, 0, pair, source[place, :, pair * 256 : pair * 256 + 256])


def step_state(z, matrix, offset, wide0, wide1, sens, weight):
    parts = products(matrix, wide0, z)
    base = pl.multiple_of((z + 1) * 384, 384)
    for pair in range(4):
        cols = slice(pair * 256, pair * 256 + 256)
        tanh = jnp.tanh(combined(parts, pair) + offset)
        sens[z, :, cols] = 1.0 - tanh * tanh
        value = wide0[pl.ds(base + 128, 128), cols].astype(f32) + STEP * tanh
        if weight is not None:
            value = value * weight
        put(wide1, z, 0, pair, value.astype(bf16))


def inner_body(spot, own_a, own_b, lam, matrix, bias, wide0, wide1, sens, factor, lam_rows, average_lam, turn):
    average = averaging()
    for base, source in zip(sides(spot), (own_a, own_b)):
        put_planes(wide0, base + 2, source)
    offset = bias[...]

    def inside(z, carry):
        step_state(z, matrix, offset, wide0, wide1, sens, None)
        return carry

    lax.fori_loop(2, 4, inside, 0, unroll=True)
    for z in range(4):
        to_rows(lam, z, turn)
        for pair in range(4):
            cols = slice(pair * 256, pair * 256 + 256)
            value = pair_of(turn, pair)
            lam_rows[z, :, cols] = value
            average_lam[z, pair] = split_dot(value[0:64] + value[64:128], average)


def forward_body(side, spot, mask, wide0_in, wide1_in, sens_in, factor_in, halo, lam, matrix, bias, diag, wide0, wide1, sens, factor, cot):
    base = sides(spot)[side]
    put_planes(wide0, 3 * base, halo)
    offset = bias[...]
    for place in range(2):
        z = 2 * base + place
        step_state(z, matrix, offset, wide0, wide1, sens, mask[z])
    average = averaging()
    cot[2] = lam[base + base // 2].astype(bf16)
    for place in range(2):
        z = base + place
        parts = products(matrix, wide1, z)
        for pair in range(4):
            cols = slice(pair * 256, pair * 256 + 256)
            tanh = jnp.tanh(combined(parts, pair) + offset)
            cot[place, :, cols] = ((1.0 - tanh * tanh) * lam[z, :, cols]).astype(bf16)
            both = sens[z + 1, 0:64, cols] + sens[z + 1, 64:128, cols]
            coarse = jnp.dot(both.astype(bf16), average, preferred_element_type=f32)
            factor[z, pair] = (coarse * diag[...]).astype(bf16)


def step_back(z, matrix, wide1, wide0, middle, sens, lam, weight):
    parts = products(matrix, wide1, z)
    for pair in range(4):
        cols = slice(pair * 256, pair * 256 + 256)
        value = lam(cols) + STEP * combined(parts, pair)
        middle[z, :, cols] = value
        value = sens[z, :, cols] * value
        if weight is not None:
            value = value * weight
        put(wide0, z, 0, pair, value.astype(bf16))


def back_inner_body(spot, own_a, own_b, lam, sens, matrix, wide1, wide0, middle):
    for base, source in zip(sides(spot), (own_a, own_b)):
        put_planes(wide1, base + 2, source)

    def inside(z, carry):
        step_back(z, matrix, wide1, wide0, middle, sens, lambda cols: lam[z - 1, :, cols], None)
        return carry

    lax.fori_loop(2, 4, inside, 0, unroll=True)


def back_outer_body(side, spot, mask, wide1_in, wide0_in, middle_in, halo, lam, sens, matrix, wide1, wide0, middle):
    base = sides(spot)[side]
    put_planes(wide1, 3 * base, halo)
    z = 1 + base + base // 2
    step_back(z, matrix, wide1, wide0, middle, sens, lambda cols: lam[z - 1, :, cols], None)
    far = 2 * base + base // 2
    step_back(far, matrix, wide1, wide0, middle, sens, lambda cols: halo[2, :, cols].astype(f32), mask[far])


def back_last_body(wide0, middle, average_lam, factor, matrix, coarse, kept):
    average = averaging()

    def last(z, carry):
        parts = products(matrix, wide0, z)
        for pair in range(4):
            cols = slice(pair * 256, pair * 256 + 256)
            value = middle[z + 1, :, cols] + STEP * combined(parts, pair)
            back = split_dot(value[0:64] + value[64:128], average)
            here = average_lam[z, pair]
            kept[z, pair] = here
            coarse[z, pair] = (back - here - factor[z, pair].astype(f32) * here).astype(bf16)
        return carry

    lax.fori_loop(0, 4, last, 0)


def gradient_body(scale, spot, *refs):
    last = len(refs) == 8
    cots, wide, rest = (refs[:1], refs[1], refs[2:]) if last else (refs[:2], refs[2], refs[3:])
    if last:
        earlier, mine, others, out, widened_cot, total = rest
    else:
        out, widened_cot, total = rest
    sums = jnp.zeros((128, 128), f32)
    zero = jnp.zeros((64, 256), bf16)
    side_a, side_b = sides(spot)
    for z in range(4):
        if last:
            value = cots[0][(z + 1) * 384 + 128 : (z + 1) * 384 + 256, :]
        else:
            value = cots[z // 2][z % 2]
        widened_cot[z, 0:128] = value
        widened_cot[z, 128:192] = jnp.concatenate([zero, value[64:128, :768]], 1)
        widened_cot[z, 192:256] = jnp.concatenate([value[0:64, 256:], zero], 1)
        for part in range(8):
            sums = sums + value[:, part * 128 : part * 128 + 128].astype(f32)
    total[...] = jnp.zeros_like(total)

    def plane(z, carry):
        above = z + 1 if last else jnp.where(z < 2, side_a, side_b) + z % 2
        base = pl.multiple_of(above * 384, 384)
        total[...] += lax.dot_general(
            widened_cot[z],
            wide[pl.ds(base, 1152), :],
            (((1,), (1,)), ((), ())),
            preferred_element_type=f32,
        )
        return carry

    lax.fori_loop(0, 4, plane, 0, unroll=True)
    lower = lax.broadcasted_iota(jnp.int32, (64, 128), 1) < 64

    def give(block, value):
        out[block] = (value + earlier[block]) * scale if last else value

    for tap in range(9):
        cols = slice(tap * 128, tap * 128 + 128)
        rows = [total[64 * q : 64 * q + 64, cols] for q in range(4)]
        taps = [jnp.where(lower, rows[1], rows[3]), jnp.where(lower, rows[0], rows[1]), jnp.where(lower, rows[2], rows[0])]
        taps = [value + pltpu.roll(value, 64, 1) for value in taps]
        give(tap, jnp.where(lower, taps[0], taps[1]))
        if tap % 2 == 0:
            kept = taps[2]
        else:
            give(9 + tap // 2, jnp.where(lower, kept, taps[2]))
    give(13, kept)
    give(14, sums[0:64] + sums[64:128])
    give(15, jnp.zeros((64, 128), f32))
    if last:
        for block in range(8):
            mine[block] = out[block + 8 * spot[0]]
            others[block] = out[block + 8 - 8 * spot[0]]


def gradient(scale, spot, cots, wide, earlier=None):
    blocks, half = pltpu.VMEM((16, 64, 128), f32), pltpu.VMEM((8, 64, 128), f32)
    ins = [*cots, wide] if earlier is None else [*cots, wide, earlier]
    return run(
        functools.partial(gradient_body, scale),
        "gradient",
        5,
        blocks if earlier is None else (half, half),
        [spot] + [near(value) for value in ins],
        ([] if earlier is None else [blocks]) + [pltpu.VMEM((4, 256, 1024), bf16), pltpu.VMEM((256, 1152), f32)],
        scalars=1,
    )


def pack_body(mine, received, coarse, factor, out):
    for group in range(out.shape[0]):
        out[group, 0:128] = coarse[group]
        out[group, 128:256] = factor[group]
        out[group, 256:320] = (mine[group] + received[group]).astype(bf16)


def meet_body(mixed, out, shared):
    groups = mixed.shape[0]
    value = jnp.zeros((128, 128), f32)
    out[0] = value.astype(bf16)
    summed = mixed[0, 256:320].astype(f32)
    for group in range(groups - 1):
        value = value + mixed[group, 128:256].astype(f32) * value + mixed[group, 0:128].astype(f32)
        out[group + 1] = value.astype(bf16)
        summed = summed + mixed[group + 1, 256:320].astype(f32)
    summed = summed.astype(bf16)
    for chip in range(shared.shape[0]):
        shared[chip] = summed


def join_body(shared, carried, out):
    summed = shared[0].astype(f32)
    for chip in range(1, shared.shape[0]):
        summed = summed + shared[chip].astype(f32)
    summed = summed.astype(bf16)
    for group in range(out.shape[0]):
        out[group, 0:128] = carried[group]
        out[group, 128:192] = summed


def finish_body(lam, average_lam, joined, out, turn):
    fine = lax.broadcasted_iota(jnp.int32, (128, 256), 1)
    coarse = lax.broadcasted_iota(jnp.int32, (128, 256), 0)
    copies = jnp.where((fine == 2 * coarse) | (fine == 2 * coarse + 1), 1.0, 0.0).astype(bf16)

    def plane(z, carry):
        for pair in range(4):
            carried = joined[2 * z + pair // 2, 64 * (pair % 2) : 64 * (pair % 2) + 64]
            value = split_dot(carried.astype(f32) - average_lam[z, pair], copies)
            for half in range(2):
                for x in (2 * pair, 2 * pair + 1):
                    turn[half, pl.ds(x, 64, stride=8), :] = value[:, half * 128 : half * 128 + 128]
        added = jnp.concatenate([turn[0], turn[1]], 1).reshape(64, 8, 256)
        out[:, z] = lam[:, z] + added
        return carry

    lax.fori_loop(0, 4, plane, 0, unroll=True)


def taps_body(spot, joined, received, taps, offset):
    def block(index):
        own = joined[index % 8, 128:192].astype(f32)
        other = received[index % 8].astype(f32)
        return jnp.where(spot[0] == index // 8, own, other)

    for a in range(3):
        for c in range(3):
            tap = 3 * a + c
            both = block(tap)
            taps[9 * a + c] = both[:, :64]
            taps[9 * a + 3 + c] = both[:, 64:]
            half = 64 * (tap % 2)
            taps[9 * a + 6 + c] = block(9 + tap // 2)[:, half : half + 64]
    row = lax.broadcasted_iota(jnp.int32, (64, 64), 0)
    col = lax.broadcasted_iota(jnp.int32, (64, 64), 1)
    column = jnp.broadcast_to(jnp.sum(block(14), axis=1, keepdims=True), (64, 64))
    offset[...] = jnp.sum(jnp.where(row == col, column, 0.0), axis=0, keepdims=True)


def prepare_body(mask, weight, bias, matrix, flipped, offset, diag):
    row = lax.broadcasted_iota(jnp.int32, (64, 64), 0)
    col = lax.broadcasted_iota(jnp.int32, (64, 64), 1)
    zero = jnp.zeros((64, 64), f32)

    def column(values):
        return jnp.sum(jnp.where(row == col, values, 0.0), axis=1, keepdims=True)

    def build(out, tap):
        for a in range(3):
            for c in range(3):
                taps = [tap(9 * a + 3 * b + c) for b in range(3)]
                sides = ((taps[1], taps[2]), (taps[0], taps[1]), (taps[2], zero), (zero, taps[0]))
                start = (3 * a + c) * 128
                for place in range(4):
                    both = jnp.concatenate(sides[place], 1)
                    out[64 * place : 64 * place + 64, start : start + 128] = both.astype(bf16)

    build(matrix, lambda tap: weight[tap].astype(f32))
    build(flipped, lambda tap: weight[26 - tap].astype(f32).T)
    column_bias = jnp.broadcast_to(column(jnp.broadcast_to(bias[...], (64, 64))), (64, 256))
    offset[0:64] = column_bias
    offset[64:128] = column_bias
    diag[...] = jnp.broadcast_to(2.0 * STEP * column(weight[13].astype(f32)), (64, 128))


def beside(value):
    return lax.ppermute(value, "slab", [(i, i ^ 1) for i in range(lax.axis_size("slab"))])


def across(value):
    up = [(i, i + 1) for i in range(1, lax.axis_size("slab") - 1, 2)]
    return lax.ppermute(value, "slab", up + [(j, i) for i, j in up])


def exchanged(value, axes):
    return lax.all_to_all(value, axes, 0, 0, tiled=True)


def on_device(u_states, lam_points, weight, bias):
    u, lam = u_states[0], lam_points[0]
    slab, slabs = lax.axis_index("slab"), lax.axis_size("slab")
    groups = lax.axis_size("tm")
    ones = jnp.ones((4,), f32)
    mask = jnp.concatenate([(slab > 0).astype(f32)[None], ones, (slab < slabs - 1).astype(f32)[None]])
    spot = (slab % 2).astype(jnp.int32)[None]
    own_b = opened(1, spot, u)
    halo_b = across(own_b)
    own_a = opened(0, spot, u)
    halo_a = beside(own_a)
    taps = pltpu.VMEM((256, 1152), bf16)
    matrix, flipped, offset, diag = run(
        prepare_body,
        "prepare",
        2,
        (taps, taps, pltpu.VMEM((128, 256), f32), pltpu.VMEM((64, 128), f32)),
        [mask, weight, bias[None]],
        scalars=1,
    )
    matrix, flipped, offset, diag = (near(v) for v in (matrix, flipped, offset, diag))
    coarse_shape = pltpu.VMEM((4, 4, 64, 128), bf16)
    average_shape = (4, 4, 64, 128)
    states = (widened(8), widened(6), field(6, f32))
    *kept, lam_rows, average_lam = run(
        inner_body,
        "inner",
        5,
        (*states, coarse_shape, field(4, f32), pltpu.VMEM(average_shape, f32)),
        [spot, near(own_a), near(own_b), lam, matrix, offset],
        [TURN],
        scalars=1,
    )

    def forward(side, kept, halo):
        return run(
            functools.partial(forward_body, side),
            "forward",
            4,
            (*states, coarse_shape, field(3, bf16)),
            [spot, mask] + [near(v) for v in (*kept, halo, lam_rows)] + [matrix, offset, diag],
            aliases={2: 0, 3: 1, 4: 2, 5: 3},
            scalars=2,
        )

    *kept, own_a = forward(0, kept, halo_a)
    cot_a = beside(own_a)
    wide0, wide1, sens, factor, own_b = forward(1, kept, halo_b)
    cot_b = across(own_b)
    scale = STEP / math.sqrt(2 * groups * slabs * 4 * 8 * 256)
    earlier = gradient(scale, spot, (own_a, own_b), wide1)
    back1, back0, middle = run(
        back_inner_body,
        "back_inner",
        3,
        (widened(8), widened(6), field(6, f32)),
        [spot] + [near(v) for v in (own_a, own_b, lam_rows, sens)] + [flipped],
        scalars=1,
    )
    kept = (back1, back0, middle)
    for side, halo in enumerate((cot_a, cot_b)):
        kept = run(
            functools.partial(back_outer_body, side),
            "back_outer",
            3,
            states,
            [spot, mask] + [near(v) for v in (*kept, halo, lam_rows, sens)] + [flipped],
            aliases={2: 0, 3: 1, 4: 2},
            scalars=2,
        )
    back1, back0, middle = kept
    mine, others = gradient(scale, spot, (back0,), wide0, earlier)
    received = beside(others)
    coarse, average_lam = run(
        back_last_body,
        "back_last",
        5,
        (coarse_shape, jax.ShapeDtypeStruct(average_shape, f32)),
        [near(v) for v in (back0, middle, average_lam, factor)] + [flipped],
    )
    pieces = (groups, 128, 128)
    mixed = run(
        pack_body,
        "pack",
        1,
        jax.ShapeDtypeStruct((groups, 320, 128), bf16),
        [near(v) for v in (mine, received, coarse.reshape(pieces), factor.reshape(pieces))],
    )
    carried, shared = run(
        meet_body,
        "meet",
        1,
        (jax.ShapeDtypeStruct(pieces, bf16), jax.ShapeDtypeStruct((slabs // 2, 64, 128), bf16)),
        [exchanged(mixed, "tm")],
    )
    same_core = [list(range(core, slabs, 2)) for core in range(2)]
    shared = lax.all_to_all(shared, "slab", 0, 0, tiled=True, axis_index_groups=same_core)
    joined = run(
        join_body,
        "join",
        1,
        jax.ShapeDtypeStruct((groups, 192, 128), bf16),
        [shared, carried],
    )
    joined = exchanged(joined, "tm")
    received = beside(joined[:, 128:])
    updated = run(
        finish_body,
        "finish",
        3,
        jax.ShapeDtypeStruct(lam.shape, f32),
        [lam, average_lam, joined],
        [TURN],
    )
    taps, offset = run(
        taps_body,
        "taps",
        1,
        (jax.ShapeDtypeStruct(weight.shape, f32), jax.ShapeDtypeStruct((1, 64), f32)),
        [spot, joined, received],
        scalars=1,
    )
    return updated[None], taps, offset[0]


def solution(mesh):
    in_specs = (P("tm", None, "slab", None, None), P("tm", None, "slab", None, None), P(), P())
    out_specs = (P("tm", None, "slab", None, None), P(), P())
    return jax.shard_map(
        on_device, mesh=mesh, in_specs=in_specs, out_specs=out_specs, check_vma=False
    )
```

```python
import functools
import math

import jax
import jax.numpy as jnp
from jax import lax
from jax.experimental import pallas as pl
from jax.experimental.pallas import tpu as pltpu
from jax.sharding import PartitionSpec as P

f32, bf16 = jnp.float32, jnp.bfloat16
STEP = 0.25


def shifts(value):
    lane = lax.broadcasted_iota(jnp.int32, value.shape, 1)
    zero = jnp.zeros((), value.dtype)
    left = jnp.where(lane == 0, zero, pltpu.roll(value, 1, 1))
    right = jnp.where(lane == 255, zero, pltpu.roll(value, 255, 1))
    return left, right


def put(wide, plane, row, pair, value):
    count = value.shape[0]
    left, right = shifts(value)
    base = pl.multiple_of(plane * 384 + row, 64)
    cols = slice(pair * 256, pair * 256 + 256)
    wide[pl.ds(base, count), cols] = left
    wide[pl.ds(base + 128, count), cols] = value
    wide[pl.ds(base + 256, count), cols] = right


def to_rows(source, z, turn):
    value = source[:, z].astype(f32).reshape(512, 256)
    turn[0] = value[:, :128]
    turn[1] = value[:, 128:]


def row_of(turn, x):
    return jnp.concatenate([turn[half, pl.ds(x, 64, stride=8), :] for half in range(2)], 1)


def pair_of(turn, pair):
    return jnp.concatenate([row_of(turn, 2 * pair), row_of(turn, 2 * pair + 1)], 0)


def products(matrix, wide, z):
    base = pl.multiple_of(z * 384, 384)
    return [
        jnp.dot(
            matrix[...],
            wide[pl.ds(base, 1152), pair * 256 : pair * 256 + 256],
            preferred_element_type=f32,
        )
        for pair in range(4)
    ]


def combined(parts, pair):
    low, high = parts[pair][0:64], parts[pair][64:128]
    if pair > 0:
        low = low + parts[pair - 1][192:256]
    if pair < 3:
        high = high + parts[pair + 1][128:192]
    return jnp.concatenate([low, high], 0)


def averaging():
    fine = lax.broadcasted_iota(jnp.int32, (256, 128), 0)
    coarse = lax.broadcasted_iota(jnp.int32, (256, 128), 1)
    return jnp.where((fine == 2 * coarse) | (fine == 2 * coarse + 1), 0.25, 0.0).astype(bf16)


def split_dot(value, matrix):
    high = value.astype(bf16)
    low = (value - high.astype(f32)).astype(bf16)
    return jnp.dot(high, matrix, preferred_element_type=f32) + jnp.dot(
        low, matrix, preferred_element_type=f32
    )


def field(planes, dtype):
    return pltpu.VMEM((planes, 128, 1024), dtype)


def widened(planes):
    return pltpu.VMEM((planes * 384, 1024), bf16)


def near(value):
    return pltpu.with_memory_space_constraint(value, pltpu.VMEM)


def run(body, name, micros, outs, ins, scratch=(), aliases=None, scalars=0, limit=8):
    in_specs = [pl.BlockSpec(memory_space=pltpu.SMEM)] * scalars
    in_specs += [pl.BlockSpec(memory_space=pltpu.VMEM)] * (len(ins) - scalars)
    return pl.pallas_call(
        body,
        out_shape=outs,
        in_specs=in_specs,
        scratch_shapes=list(scratch),
        input_output_aliases=aliases or {},
        compiler_params=pltpu.CompilerParams(vmem_limit_bytes=limit * 2**20),
        cost_estimate=pl.CostEstimate(flops=int(micros * 1e8), bytes_accessed=0, transcendentals=0),
        name=name,
    )(*ins)


TURN = pltpu.VMEM((2, 512, 128), f32)


def sides(odd):
    return 2 * (1 - odd), 2 * odd


def by_parity(body):
    def kernel(spot, *refs):
        for odd in range(2):
            pl.when(spot[0] == odd)(functools.partial(body, odd, *refs))

    return kernel


def open_body(side, odd, u, out, planes, turn, arrived):
    base = sides(odd)[side]
    copy = pltpu.make_async_copy(u.at[:, pl.ds(base, 2)], planes, arrived)
    copy.start()
    copy.wait()
    for place in range(2):
        to_rows(planes, place, turn)
        for pair in range(4):
            out[place, :, pair * 256 : pair * 256 + 256] = pair_of(turn, pair).astype(bf16)


def opened(side, spot, u):
    return pl.pallas_call(
        by_parity(functools.partial(open_body, side)),
        out_shape=field(2, bf16),
        in_specs=[pl.BlockSpec(memory_space=pltpu.SMEM), pl.BlockSpec(memory_space=pltpu.HBM)],
        scratch_shapes=[pltpu.VMEM((64, 2, 8, 256), bf16), TURN, pltpu.SemaphoreType.DMA(())],
        compiler_params=pltpu.CompilerParams(vmem_limit_bytes=8 * 2**20),
        cost_estimate=pl.CostEstimate(flops=10**8, bytes_accessed=0, transcendentals=0),
        name="open",
    )(spot, u)


def put_planes(wide, z, source):
    for place in range(2):
        for pair in range(4):
            put(wide, z + place, 0, pair, source[place, :, pair * 256 : pair * 256 + 256])


def step_state(z, matrix, offset, wide0, wide1, sens, weight):
    parts = products(matrix, wide0, z)
    base = pl.multiple_of((z + 1) * 384, 384)
    for pair in range(4):
        cols = slice(pair * 256, pair * 256 + 256)
        tanh = jnp.tanh(combined(parts, pair) + offset)
        sens[z, :, cols] = 1.0 - tanh * tanh
        value = wide0[pl.ds(base + 128, 128), cols].astype(f32) + STEP * tanh
        if weight is not None:
            value = value * weight
        put(wide1, z, 0, pair, value.astype(bf16))


def inner_body(odd, own_a, own_b, lam, matrix, bias, wide0, wide1, sens, factor, lam_rows, average_lam, turn):
    average = averaging()
    for base, source in zip(sides(odd), (own_a, own_b)):
        put_planes(wide0, base + 2, source)
    offset = bias[...]

    def inside(z, carry):
        step_state(z, matrix, offset, wide0, wide1, sens, None)
        return carry

    lax.fori_loop(2, 4, inside, 0, unroll=True)
    for z in range(4):
        to_rows(lam, z, turn)
        for pair in range(4):
            cols = slice(pair * 256, pair * 256 + 256)
            value = pair_of(turn, pair)
            lam_rows[z, :, cols] = value
            average_lam[z, pair] = split_dot(value[0:64] + value[64:128], average)


def forward_body(side, odd, mask, wide0_in, wide1_in, sens_in, factor_in, halo, lam, matrix, bias, diag, wide0, wide1, sens, factor, cot):
    base = sides(odd)[side]
    put_planes(wide0, 3 * base, halo)
    offset = bias[...]
    for place in range(2):
        z = 2 * base + place
        step_state(z, matrix, offset, wide0, wide1, sens, mask[z])
    average = averaging()
    cot[2] = lam[base + base // 2].astype(bf16)
    for place in range(2):
        z = base + place
        parts = products(matrix, wide1, z)
        for pair in range(4):
            cols = slice(pair * 256, pair * 256 + 256)
            tanh = jnp.tanh(combined(parts, pair) + offset)
            cot[place, :, cols] = ((1.0 - tanh * tanh) * lam[z, :, cols]).astype(bf16)
            both = sens[z + 1, 0:64, cols] + sens[z + 1, 64:128, cols]
            coarse = jnp.dot(both.astype(bf16), average, preferred_element_type=f32)
            factor[z, pair] = (coarse * diag[...]).astype(bf16)


def step_back(z, matrix, wide1, wide0, middle, sens, lam, weight):
    parts = products(matrix, wide1, z)
    for pair in range(4):
        cols = slice(pair * 256, pair * 256 + 256)
        value = lam(cols) + STEP * combined(parts, pair)
        middle[z, :, cols] = value
        value = sens[z, :, cols] * value
        if weight is not None:
            value = value * weight
        put(wide0, z, 0, pair, value.astype(bf16))


def back_inner_body(odd, own_a, own_b, lam, sens, matrix, wide1, wide0, middle):
    for base, source in zip(sides(odd), (own_a, own_b)):
        put_planes(wide1, base + 2, source)

    def inside(z, carry):
        step_back(z, matrix, wide1, wide0, middle, sens, lambda cols: lam[z - 1, :, cols], None)
        return carry

    lax.fori_loop(2, 4, inside, 0, unroll=True)


def back_outer_body(side, odd, mask, wide1_in, wide0_in, middle_in, halo, lam, sens, matrix, *refs):
    wide1, wide0, middle = refs[-3:]
    base = sides(odd)[side]
    put_planes(wide1, 3 * base, halo)
    z = 1 + base + base // 2
    step_back(z, matrix, wide1, wide0, middle, sens, lambda cols: lam[z - 1, :, cols], None)
    far = 2 * base + base // 2
    step_back(far, matrix, wide1, wide0, middle, sens, lambda cols: halo[2, :, cols].astype(f32), mask[far])


def back_last_body(side, odd, *refs):
    wide0, middle, average_lam, factor, matrix = refs[:5]
    coarse, average = refs[-1 - side], averaging()
    base = sides(odd)[side]

    def last(place, carry):
        z = base + place
        parts = products(matrix, wide0, z)
        for pair in range(4):
            cols = slice(pair * 256, pair * 256 + 256)
            value = middle[z + 1, :, cols] + STEP * combined(parts, pair)
            back = split_dot(value[0:64] + value[64:128], average)
            here = average_lam[z, pair]
            coarse[z, pair] = (back - here - factor[z, pair].astype(f32) * here).astype(bf16)
        return carry

    lax.fori_loop(0, 2, last, 0)
    if side:
        refs[-1][...] = average_lam[...]


def add_plane(cot, wide, z, widened_cot, total, sums):
    zero = jnp.zeros((64, 256), bf16)
    widened_cot[0:128] = cot
    widened_cot[128:192] = jnp.concatenate([zero, cot[64:128, :768]], 1)
    widened_cot[192:256] = jnp.concatenate([cot[0:64, 256:], zero], 1)
    total[...] += lax.dot_general(
        widened_cot[...],
        wide[pl.ds(pl.multiple_of(z * 384, 384), 1152), :],
        (((1,), (1,)), ((), ())),
        preferred_element_type=f32,
    )
    for part in range(8):
        sums[...] += cot[:, part * 128 : part * 128 + 128].astype(f32)


def centre(back0, z):
    return back0[pl.ds(pl.multiple_of((z + 1) * 384 + 128, 128), 128), :]


def gradient_first_body(odd, own_a, own_b, wide1, back0, wide0, total, sums, widened_cot):
    total[...] = jnp.zeros_like(total)
    sums[...] = jnp.zeros_like(sums)
    index = 0
    for base, source in zip(sides(odd), (own_a, own_b)):
        for place in range(2):
            add_plane(source[place], wide1, base + place, widened_cot.at[index], total, sums)
            index += 1
    for z in range(1 - odd, 4 - odd):
        add_plane(centre(back0, z), wide0, z + 1, widened_cot.at[index], total, sums)
        index += 1


def gradient_last_body(scale, spot, back0, wide0, total_in, sums_in, total, sums, mine, others, out, widened_cot):
    z = 3 * spot[0]
    add_plane(centre(back0, z), wide0, z + 1, widened_cot, total, sums)
    lower = lax.broadcasted_iota(jnp.int32, (64, 128), 1) < 64
    for tap in range(9):
        cols = slice(tap * 128, tap * 128 + 128)
        rows = [total[64 * q : 64 * q + 64, cols] * scale for q in range(4)]
        taps = [jnp.where(lower, rows[1], rows[3]), jnp.where(lower, rows[0], rows[1]), jnp.where(lower, rows[2], rows[0])]
        taps = [value + pltpu.roll(value, 64, 1) for value in taps]
        out[tap] = jnp.where(lower, taps[0], taps[1])
        if tap % 2 == 0:
            kept = taps[2]
        else:
            out[9 + tap // 2] = jnp.where(lower, kept, taps[2])
    out[13] = kept
    out[14] = (sums[0:64] + sums[64:128]) * scale
    out[15] = jnp.zeros((64, 128), f32)
    for block in range(8):
        mine[block] = out[block + 8 * spot[0]]
        others[block] = out[block + 8 - 8 * spot[0]]


def pack_body(mine, received, coarse, factor, out):
    for group in range(out.shape[0]):
        out[group, 0:128] = coarse[group]
        out[group, 128:256] = factor[group]
        out[group, 256:320] = (mine[group] + received[group]).astype(bf16)


def meet_body(mixed, out, shared):
    groups = mixed.shape[0]
    value = jnp.zeros((128, 128), f32)
    out[0] = value.astype(bf16)
    summed = mixed[0, 256:320].astype(f32)
    for group in range(groups - 1):
        value = value + mixed[group, 128:256].astype(f32) * value + mixed[group, 0:128].astype(f32)
        out[group + 1] = value.astype(bf16)
        summed = summed + mixed[group + 1, 256:320].astype(f32)
    summed = summed.astype(bf16)
    for chip in range(shared.shape[0]):
        shared[chip] = summed


def join_body(shared, carried, out):
    summed = shared[0].astype(f32)
    for chip in range(1, shared.shape[0]):
        summed = summed + shared[chip].astype(f32)
    summed = summed.astype(bf16)
    for group in range(out.shape[0]):
        out[group, 0:128] = carried[group]
        out[group, 128:192] = summed


def finish_body(lam, average_lam, joined, out, turn):
    fine = lax.broadcasted_iota(jnp.int32, (128, 256), 1)
    coarse = lax.broadcasted_iota(jnp.int32, (128, 256), 0)
    copies = jnp.where((fine == 2 * coarse) | (fine == 2 * coarse + 1), 1.0, 0.0).astype(bf16)

    def plane(z, carry):
        for pair in range(4):
            carried = joined[2 * z + pair // 2, 64 * (pair % 2) : 64 * (pair % 2) + 64]
            value = split_dot(carried.astype(f32) - average_lam[z, pair], copies)
            for half in range(2):
                for x in (2 * pair, 2 * pair + 1):
                    turn[half, pl.ds(x, 64, stride=8), :] = value[:, half * 128 : half * 128 + 128]
        added = jnp.concatenate([turn[0], turn[1]], 1).reshape(64, 8, 256)
        out[:, z] = lam[:, z] + added
        return carry

    lax.fori_loop(0, 4, plane, 0, unroll=True)


def taps_body(spot, joined, received, taps, offset):
    def block(index):
        own = joined[index % 8, 128:192].astype(f32)
        other = received[index % 8].astype(f32)
        return jnp.where(spot[0] == index // 8, own, other)

    for a in range(3):
        for c in range(3):
            tap = 3 * a + c
            both = block(tap)
            taps[9 * a + c] = both[:, :64]
            taps[9 * a + 3 + c] = both[:, 64:]
            half = 64 * (tap % 2)
            taps[9 * a + 6 + c] = block(9 + tap // 2)[:, half : half + 64]
    row = lax.broadcasted_iota(jnp.int32, (64, 64), 0)
    col = lax.broadcasted_iota(jnp.int32, (64, 64), 1)
    column = jnp.broadcast_to(jnp.sum(block(14), axis=1, keepdims=True), (64, 64))
    offset[...] = jnp.sum(jnp.where(row == col, column, 0.0), axis=0, keepdims=True)


def prepare_body(mask, weight, bias, matrix, flipped, offset, diag):
    row = lax.broadcasted_iota(jnp.int32, (64, 64), 0)
    col = lax.broadcasted_iota(jnp.int32, (64, 64), 1)
    zero = jnp.zeros((64, 64), f32)

    def column(values):
        return jnp.sum(jnp.where(row == col, values, 0.0), axis=1, keepdims=True)

    def build(out, tap):
        for a in range(3):
            for c in range(3):
                taps = [tap(9 * a + 3 * b + c) for b in range(3)]
                sides = ((taps[1], taps[2]), (taps[0], taps[1]), (taps[2], zero), (zero, taps[0]))
                start = (3 * a + c) * 128
                for place in range(4):
                    both = jnp.concatenate(sides[place], 1)
                    out[64 * place : 64 * place + 64, start : start + 128] = both.astype(bf16)

    build(matrix, lambda tap: weight[tap].astype(f32))
    build(flipped, lambda tap: weight[26 - tap].astype(f32).T)
    column_bias = jnp.broadcast_to(column(jnp.broadcast_to(bias[...], (64, 64))), (64, 256))
    offset[0:64] = column_bias
    offset[64:128] = column_bias
    diag[...] = jnp.broadcast_to(2.0 * STEP * column(weight[13].astype(f32)), (64, 128))


def beside(value):
    return lax.ppermute(value, "slab", [(i, i ^ 1) for i in range(lax.axis_size("slab"))])


def across(value):
    up = [(i, i + 1) for i in range(1, lax.axis_size("slab") - 1, 2)]
    return lax.ppermute(value, "slab", up + [(j, i) for i, j in up])


def exchanged(value, axes):
    return lax.all_to_all(value, axes, 0, 0, tiled=True)


def on_device(u_states, lam_points, weight, bias):
    u, lam = u_states[0], lam_points[0]
    slab, slabs = lax.axis_index("slab"), lax.axis_size("slab")
    groups = lax.axis_size("tm")
    ones = jnp.ones((4,), f32)
    mask = jnp.concatenate([(slab > 0).astype(f32)[None], ones, (slab < slabs - 1).astype(f32)[None]])
    spot = (slab % 2).astype(jnp.int32)[None]
    own_b = opened(1, spot, u)
    halo_b = across(own_b)
    own_a = opened(0, spot, u)
    halo_a = beside(own_a)
    taps = pltpu.VMEM((256, 1152), bf16)
    matrix, flipped, offset, diag = run(
        prepare_body,
        "prepare",
        2,
        (taps, taps, pltpu.VMEM((128, 256), f32), pltpu.VMEM((64, 128), f32)),
        [mask, weight, bias[None]],
        scalars=1,
    )
    matrix, flipped, offset, diag = (near(v) for v in (matrix, flipped, offset, diag))
    coarse_shape = pltpu.VMEM((4, 4, 64, 128), bf16)
    average_shape = (4, 4, 64, 128)
    states = (widened(8), widened(6), field(6, f32))
    *kept, lam_rows, average_lam = run(
        by_parity(inner_body),
        "inner",
        5,
        (*states, coarse_shape, field(4, f32), pltpu.VMEM(average_shape, f32)),
        [spot, near(own_a), near(own_b), lam, matrix, offset],
        [TURN],
        scalars=1,
    )

    def forward(side, kept, halo):
        return run(
            by_parity(functools.partial(forward_body, side)),
            "forward",
            4,
            (*states, coarse_shape, field(3, bf16)),
            [spot, mask] + [near(v) for v in (*kept, halo, lam_rows)] + [matrix, offset, diag],
            aliases={2: 0, 3: 1, 4: 2, 5: 3},
            scalars=2,
        )

    *kept, own_a = forward(0, kept, halo_a)
    cot_a = beside(own_a)
    wide0, wide1, sens, factor, own_b = forward(1, kept, halo_b)
    cot_b = across(own_b)
    scale = STEP / math.sqrt(2 * groups * slabs * 4 * 8 * 256)
    back1, back0, middle = run(
        by_parity(back_inner_body),
        "back_inner",
        3,
        (widened(8), widened(6), field(6, f32)),
        [spot] + [near(v) for v in (own_a, own_b, lam_rows, sens)] + [flipped],
        scalars=1,
    )
    def back_outer(side, kept, halo, *after):
        return run(
            by_parity(functools.partial(back_outer_body, side)),
            "back_outer",
            3,
            states,
            [spot, mask] + [near(v) for v in (*kept, halo, lam_rows, sens)] + [flipped] + [near(v) for v in after],
            aliases={2: 0, 3: 1, 4: 2},
            scalars=2,
        )

    def back_last(side, *earlier):
        outs = (coarse_shape, jax.ShapeDtypeStruct(average_shape, f32)) if side else coarse_shape
        return run(
            by_parity(functools.partial(back_last_body, side)),
            "back_last",
            2,
            outs,
            [spot] + [near(v) for v in (back0, middle, average_lam, factor)] + [flipped] + [near(v) for v in earlier],
            aliases={6: 0} if side else None,
            scalars=1,
        )

    back1, back0, middle = back_outer(0, (back1, back0, middle), cot_a)
    sums_shapes = (pltpu.VMEM((256, 1152), f32), pltpu.VMEM((128, 128), f32))
    total, sums = run(
        by_parity(gradient_first_body),
        "gradient_first",
        5,
        sums_shapes,
        [spot] + [near(v) for v in (own_a, own_b, wide1, back0, wide0)],
        [pltpu.VMEM((7, 256, 1024), bf16)],
        scalars=1,
    )
    coarse = back_last(0)
    back1, back0, middle = back_outer(1, (back1, back0, middle), cot_b, sums, coarse)
    half = pltpu.VMEM((8, 64, 128), f32)
    _, _, mine, others = run(
        functools.partial(gradient_last_body, scale),
        "gradient_last",
        2,
        (*sums_shapes, half, half),
        [spot] + [near(v) for v in (back0, wide0, total, sums)],
        [pltpu.VMEM((16, 64, 128), f32), pltpu.VMEM((256, 1024), bf16)],
        aliases={3: 0, 4: 1},
        scalars=1,
    )
    received = beside(others)
    coarse, average_lam = back_last(1, coarse)
    pieces = (groups, 128, 128)
    mixed = run(
        pack_body,
        "pack",
        1,
        jax.ShapeDtypeStruct((groups, 320, 128), bf16),
        [near(v) for v in (mine, received, coarse.reshape(pieces), factor.reshape(pieces))],
    )
    carried, shared = run(
        meet_body,
        "meet",
        1,
        (jax.ShapeDtypeStruct(pieces, bf16), jax.ShapeDtypeStruct((slabs // 2, 64, 128), bf16)),
        [exchanged(mixed, "tm")],
    )
    same_core = [list(range(core, slabs, 2)) for core in range(2)]
    shared = lax.all_to_all(shared, "slab", 0, 0, tiled=True, axis_index_groups=same_core)
    joined = run(
        join_body,
        "join",
        1,
        jax.ShapeDtypeStruct((groups, 192, 128), bf16),
        [shared, carried],
    )
    joined = exchanged(joined, "tm")
    received = beside(joined[:, 128:])
    updated = run(
        finish_body,
        "finish",
        3,
        jax.ShapeDtypeStruct(lam.shape, f32),
        [lam, average_lam, joined],
        [TURN],
    )
    taps, offset = run(
        taps_body,
        "taps",
        1,
        (jax.ShapeDtypeStruct(weight.shape, f32), jax.ShapeDtypeStruct((1, 64), f32)),
        [spot, joined, received],
        scalars=1,
    )
    return updated[None], taps, offset[0]


def solution(mesh):
    in_specs = (P("tm", None, "slab", None, None), P("tm", None, "slab", None, None), P(), P())
    out_specs = (P("tm", None, "slab", None, None), P(), P())
    return jax.shard_map(
        on_device, mesh=mesh, in_specs=in_specs, out_specs=out_specs, check_vma=False
    )
```

```python
import functools
import math

import jax
import jax.numpy as jnp
from jax import lax
from jax.experimental import pallas as pl
from jax.experimental.pallas import tpu as pltpu
from jax.sharding import PartitionSpec as P

f32, bf16 = jnp.float32, jnp.bfloat16
STEP = 0.25


def shifts(value):
    lane = lax.broadcasted_iota(jnp.int32, value.shape, 1)
    zero = jnp.zeros((), value.dtype)
    left = jnp.where(lane == 0, zero, pltpu.roll(value, 1, 1))
    right = jnp.where(lane == 255, zero, pltpu.roll(value, 255, 1))
    return left, right


def put(wide, plane, row, pair, value):
    count = value.shape[0]
    left, right = shifts(value)
    base = pl.multiple_of(plane * 384 + row, 64)
    cols = slice(pair * 256, pair * 256 + 256)
    wide[pl.ds(base, count), cols] = left
    wide[pl.ds(base + 128, count), cols] = value
    wide[pl.ds(base + 256, count), cols] = right


def to_rows(source, z, turn):
    value = source[:, z].astype(f32).reshape(512, 256)
    turn[0] = value[:, :128]
    turn[1] = value[:, 128:]


def row_of(turn, x):
    return jnp.concatenate([turn[half, pl.ds(x, 64, stride=8), :] for half in range(2)], 1)


def pair_of(turn, pair):
    return jnp.concatenate([row_of(turn, 2 * pair), row_of(turn, 2 * pair + 1)], 0)


def products(matrix, wide, z):
    base = pl.multiple_of(z * 384, 384)
    return [
        jnp.dot(
            matrix[...],
            wide[pl.ds(base, 1152), pair * 256 : pair * 256 + 256],
            preferred_element_type=f32,
        )
        for pair in range(4)
    ]


def combined(parts, pair):
    low, high = parts[pair][0:64], parts[pair][64:128]
    if pair > 0:
        low = low + parts[pair - 1][192:256]
    if pair < 3:
        high = high + parts[pair + 1][128:192]
    return jnp.concatenate([low, high], 0)


def averaging():
    fine = lax.broadcasted_iota(jnp.int32, (256, 128), 0)
    coarse = lax.broadcasted_iota(jnp.int32, (256, 128), 1)
    return jnp.where((fine == 2 * coarse) | (fine == 2 * coarse + 1), 0.25, 0.0).astype(bf16)


def split_dot(value, matrix):
    high = value.astype(bf16)
    low = (value - high.astype(f32)).astype(bf16)
    return jnp.dot(high, matrix, preferred_element_type=f32) + jnp.dot(
        low, matrix, preferred_element_type=f32
    )


def field(planes, dtype):
    return pltpu.VMEM((planes, 128, 1024), dtype)


def widened(planes):
    return pltpu.VMEM((planes * 384, 1024), bf16)


def near(value):
    return pltpu.with_memory_space_constraint(value, pltpu.VMEM)


def run(body, name, micros, outs, ins, scratch=(), aliases=None, scalars=0, limit=8):
    in_specs = [pl.BlockSpec(memory_space=pltpu.SMEM)] * scalars
    in_specs += [pl.BlockSpec(memory_space=pltpu.VMEM)] * (len(ins) - scalars)
    return pl.pallas_call(
        body,
        out_shape=outs,
        in_specs=in_specs,
        scratch_shapes=list(scratch),
        input_output_aliases=aliases or {},
        compiler_params=pltpu.CompilerParams(vmem_limit_bytes=limit * 2**20),
        cost_estimate=pl.CostEstimate(flops=int(micros * 1e8), bytes_accessed=0, transcendentals=0),
        name=name,
    )(*ins)


TURN = pltpu.VMEM((2, 512, 128), f32)


def by_half(body):
    def kernel(half, *refs):
        for known in range(2):
            pl.when(half[0] == known)(functools.partial(body, 2 * known, *refs))

    return kernel


def own_plane(half_b, own_a, own_b, z):
    return jnp.where(half_b[0] == z // 2, own_b[z % 2], own_a[z % 2])


def open_body(half, u, out, planes, turn, arrived):
    copy = pltpu.make_async_copy(u.at[:, pl.ds(2 * half[0], 2)], planes, arrived)
    copy.start()
    copy.wait()
    for place in range(2):
        to_rows(planes, place, turn)
        for pair in range(4):
            out[place, :, pair * 256 : pair * 256 + 256] = pair_of(turn, pair).astype(bf16)


def opened(half, u):
    return pl.pallas_call(
        open_body,
        out_shape=field(2, bf16),
        in_specs=[pl.BlockSpec(memory_space=pltpu.SMEM), pl.BlockSpec(memory_space=pltpu.HBM)],
        scratch_shapes=[pltpu.VMEM((64, 2, 8, 256), bf16), TURN, pltpu.SemaphoreType.DMA(())],
        compiler_params=pltpu.CompilerParams(vmem_limit_bytes=8 * 2**20),
        cost_estimate=pl.CostEstimate(flops=10**8, bytes_accessed=0, transcendentals=0),
        name="open",
    )(half, u)


def put_plane(wide, z, value):
    for pair in range(4):
        put(wide, z, 0, pair, value[:, pair * 256 : pair * 256 + 256])


def step_state(z, matrix, offset, wide0, wide1, sens, weight):
    parts = products(matrix, wide0, z)
    base = pl.multiple_of((z + 1) * 384, 384)
    for pair in range(4):
        cols = slice(pair * 256, pair * 256 + 256)
        tanh = jnp.tanh(combined(parts, pair) + offset)
        sens[z, :, cols] = 1.0 - tanh * tanh
        value = wide0[pl.ds(base + 128, 128), cols].astype(f32) + STEP * tanh
        if weight is not None:
            value = value * weight
        put(wide1, z, 0, pair, value.astype(bf16))


def inner_body(half_b, own_a, own_b, lam, matrix, bias, wide0, wide1, sens, factor, lam_rows, average_lam, turn):
    average = averaging()
    for z in range(4):
        put_plane(wide0, z + 2, own_plane(half_b, own_a, own_b, z))
    offset = bias[...]

    def inside(z, carry):
        step_state(z, matrix, offset, wide0, wide1, sens, None)
        return carry

    lax.fori_loop(2, 4, inside, 0, unroll=True)
    def lam_plane(z, carry):
        to_rows(lam, z, turn)
        for pair in range(4):
            cols = slice(pair * 256, pair * 256 + 256)
            value = pair_of(turn, pair)
            lam_rows[z, :, cols] = value
            average_lam[z, pair] = split_dot(value[0:64] + value[64:128], average)
        return carry

    lax.fori_loop(0, 4, lam_plane, 0)


def forward_body(base, mask, wide0_in, wide1_in, sens_in, factor_in, halo, lam, matrix, bias, diag, wide0, wide1, sens, factor, cot):
    for place in range(2):
        put_plane(wide0, 3 * base + place, halo[place])
    offset = bias[...]
    for place in range(2):
        z = 2 * base + place
        step_state(z, matrix, offset, wide0, wide1, sens, mask[z])
    average = averaging()
    cot[2] = lam[base + base // 2].astype(bf16)
    for place in range(2):
        z = base + place
        parts = products(matrix, wide1, z)
        for pair in range(4):
            cols = slice(pair * 256, pair * 256 + 256)
            tanh = jnp.tanh(combined(parts, pair) + offset)
            cot[place, :, cols] = ((1.0 - tanh * tanh) * lam[z, :, cols]).astype(bf16)
            both = sens[z + 1, 0:64, cols] + sens[z + 1, 64:128, cols]
            coarse = jnp.dot(both.astype(bf16), average, preferred_element_type=f32)
            factor[z, pair] = (coarse * diag[...]).astype(bf16)


def step_back(z, matrix, wide1, wide0, middle, sens, lam, weight):
    parts = products(matrix, wide1, z)
    for pair in range(4):
        cols = slice(pair * 256, pair * 256 + 256)
        value = lam(cols) + STEP * combined(parts, pair)
        middle[z, :, cols] = value
        value = sens[z, :, cols] * value
        if weight is not None:
            value = value * weight
        put(wide0, z, 0, pair, value.astype(bf16))


def back_inner_body(half_b, own_a, own_b, lam, sens, matrix, wide1, wide0, middle, blank, blank_sums):
    for z in range(4):
        put_plane(wide1, z + 2, own_plane(half_b, own_a, own_b, z))

    def inside(z, carry):
        step_back(z, matrix, wide1, wide0, middle, sens, lambda cols: lam[z - 1, :, cols], None)
        return carry

    lax.fori_loop(2, 4, inside, 0, unroll=True)


def back_outer_body(base, mask, wide1_in, wide0_in, middle_in, halo, lam, sens, matrix, *refs):
    wide1, wide0, middle = refs[-3:]
    for place in range(2):
        put_plane(wide1, 3 * base + place, halo[place])
    z = 1 + base + base // 2
    step_back(z, matrix, wide1, wide0, middle, sens, lambda cols: lam[z - 1, :, cols], None)
    far = 2 * base + base // 2
    step_back(far, matrix, wide1, wide0, middle, sens, lambda cols: halo[2, :, cols].astype(f32), mask[far])


def back_last_body(half, wide0, middle, average_lam, factor, matrix, coarse_in, coarse):
    average = averaging()

    def last(place, carry):
        z = 2 * half[0] + place
        parts = products(matrix, wide0, z)
        for pair in range(4):
            cols = slice(pair * 256, pair * 256 + 256)
            value = middle[z + 1, :, cols] + STEP * combined(parts, pair)
            back = split_dot(value[0:64] + value[64:128], average)
            here = average_lam[z, pair]
            coarse[z, pair] = (back - here - factor[z, pair].astype(f32) * here).astype(bf16)
        return carry

    lax.fori_loop(0, 2, last, 0)


def add_plane(cot, wide, z, widened_cot, total, sums):
    zero = jnp.zeros((64, 256), bf16)
    widened_cot[0:128] = cot
    widened_cot[128:192] = jnp.concatenate([zero, cot[64:128, :768]], 1)
    widened_cot[192:256] = jnp.concatenate([cot[0:64, 256:], zero], 1)
    total[...] += lax.dot_general(
        widened_cot[...],
        wide[pl.ds(pl.multiple_of(z * 384, 384), 1152), :],
        (((1,), (1,)), ((), ())),
        preferred_element_type=f32,
    )
    for part in range(8):
        sums[...] += cot[:, part * 128 : part * 128 + 128].astype(f32)


def centre(back0, z):
    return back0[pl.ds(pl.multiple_of((z + 1) * 384 + 128, 128), 128), :]


def gradient_first_body(half_b, own_a, own_b, wide1, back0, wide0, total, sums, widened_cot):
    total[...] = jnp.zeros_like(total)
    sums[...] = jnp.zeros_like(sums)
    for z in range(4):
        add_plane(own_plane(half_b, own_a, own_b, z), wide1, z, widened_cot.at[z], total, sums)
    for index in range(3):
        z = index + 1 - half_b[0]
        add_plane(centre(back0, z), wide0, z + 1, widened_cot.at[4 + index], total, sums)


def gradient_last_body(scale, spot, back0, wide0, total_in, sums_in, total, sums, mine, others, out, widened_cot):
    z = 3 * spot[0]
    add_plane(centre(back0, z), wide0, z + 1, widened_cot, total, sums)
    lower = lax.broadcasted_iota(jnp.int32, (64, 128), 1) < 64
    for tap in range(9):
        cols = slice(tap * 128, tap * 128 + 128)
        rows = [total[64 * q : 64 * q + 64, cols] * scale for q in range(4)]
        taps = [jnp.where(lower, rows[1], rows[3]), jnp.where(lower, rows[0], rows[1]), jnp.where(lower, rows[2], rows[0])]
        taps = [value + pltpu.roll(value, 64, 1) for value in taps]
        out[tap] = jnp.where(lower, taps[0], taps[1])
        if tap % 2 == 0:
            kept = taps[2]
        else:
            out[9 + tap // 2] = jnp.where(lower, kept, taps[2])
    out[13] = kept
    out[14] = (sums[0:64] + sums[64:128]) * scale
    out[15] = jnp.zeros((64, 128), f32)
    for block in range(8):
        mine[block] = out[block + 8 * spot[0]]
        others[block] = out[block + 8 - 8 * spot[0]]


def pack_body(mine, received, coarse, factor, average_lam, out, kept):
    kept[...] = average_lam[...]
    for group in range(out.shape[0]):
        out[group, 0:128] = coarse[group]
        out[group, 128:256] = factor[group]
        out[group, 256:320] = (mine[group] + received[group]).astype(bf16)


def meet_body(mixed, out, shared):
    groups = mixed.shape[0]
    value = jnp.zeros((128, 128), f32)
    out[0] = value.astype(bf16)
    summed = mixed[0, 256:320].astype(f32)
    for group in range(groups - 1):
        value = value + mixed[group, 128:256].astype(f32) * value + mixed[group, 0:128].astype(f32)
        out[group + 1] = value.astype(bf16)
        summed = summed + mixed[group + 1, 256:320].astype(f32)
    summed = summed.astype(bf16)
    for chip in range(shared.shape[0]):
        shared[chip] = summed


def join_body(shared, carried, out):
    summed = shared[0].astype(f32)
    for chip in range(1, shared.shape[0]):
        summed = summed + shared[chip].astype(f32)
    summed = summed.astype(bf16)
    for group in range(out.shape[0]):
        out[group, 0:128] = carried[group]
        out[group, 128:192] = summed


def finish_body(lam, average_lam, joined, out, turn):
    fine = lax.broadcasted_iota(jnp.int32, (128, 256), 1)
    coarse = lax.broadcasted_iota(jnp.int32, (128, 256), 0)
    copies = jnp.where((fine == 2 * coarse) | (fine == 2 * coarse + 1), 1.0, 0.0).astype(bf16)

    def plane(z, carry):
        for pair in range(4):
            carried = joined[2 * z + pair // 2, 64 * (pair % 2) : 64 * (pair % 2) + 64]
            value = split_dot(carried.astype(f32) - average_lam[z, pair], copies)
            for half in range(2):
                for x in (2 * pair, 2 * pair + 1):
                    turn[half, pl.ds(x, 64, stride=8), :] = value[:, half * 128 : half * 128 + 128]
        added = jnp.concatenate([turn[0], turn[1]], 1).reshape(64, 8, 256)
        out[:, z] = lam[:, z] + added
        return carry

    lax.fori_loop(0, 4, plane, 0, unroll=True)


def taps_body(spot, joined, received, taps, offset):
    def block(index):
        own = joined[index % 8, 128:192].astype(f32)
        other = received[index % 8].astype(f32)
        return jnp.where(spot[0] == index // 8, own, other)

    for a in range(3):
        for c in range(3):
            tap = 3 * a + c
            both = block(tap)
            taps[9 * a + c] = both[:, :64]
            taps[9 * a + 3 + c] = both[:, 64:]
            half = 64 * (tap % 2)
            taps[9 * a + 6 + c] = block(9 + tap // 2)[:, half : half + 64]
    row = lax.broadcasted_iota(jnp.int32, (64, 64), 0)
    col = lax.broadcasted_iota(jnp.int32, (64, 64), 1)
    column = jnp.broadcast_to(jnp.sum(block(14), axis=1, keepdims=True), (64, 64))
    offset[...] = jnp.sum(jnp.where(row == col, column, 0.0), axis=0, keepdims=True)


def prepare_body(mask, weight, bias, matrix, flipped, offset, diag):
    row = lax.broadcasted_iota(jnp.int32, (64, 64), 0)
    col = lax.broadcasted_iota(jnp.int32, (64, 64), 1)
    zero = jnp.zeros((64, 64), f32)

    def column(values):
        return jnp.sum(jnp.where(row == col, values, 0.0), axis=1, keepdims=True)

    def build(out, tap):
        for a in range(3):
            for c in range(3):
                taps = [tap(9 * a + 3 * b + c) for b in range(3)]
                sides = ((taps[1], taps[2]), (taps[0], taps[1]), (taps[2], zero), (zero, taps[0]))
                start = (3 * a + c) * 128
                for place in range(4):
                    both = jnp.concatenate(sides[place], 1)
                    out[64 * place : 64 * place + 64, start : start + 128] = both.astype(bf16)

    build(matrix, lambda tap: weight[tap].astype(f32))
    build(flipped, lambda tap: weight[26 - tap].astype(f32).T)
    column_bias = jnp.broadcast_to(column(jnp.broadcast_to(bias[...], (64, 64))), (64, 256))
    offset[0:64] = column_bias
    offset[64:128] = column_bias
    diag[...] = jnp.broadcast_to(2.0 * STEP * column(weight[13].astype(f32)), (64, 128))


def beside(value):
    return lax.ppermute(value, "slab", [(i, i ^ 1) for i in range(lax.axis_size("slab"))])


def across(value):
    up = [(i, i + 1) for i in range(1, lax.axis_size("slab") - 1, 2)]
    return lax.ppermute(value, "slab", up + [(j, i) for i, j in up])


def exchanged(value, axes):
    return lax.all_to_all(value, axes, 0, 0, tiled=True)


def on_device(u_states, lam_points, weight, bias):
    u, lam = u_states[0], lam_points[0]
    slab, slabs = lax.axis_index("slab"), lax.axis_size("slab")
    groups = lax.axis_size("tm")
    ones = jnp.ones((4,), f32)
    mask = jnp.concatenate([(slab > 0).astype(f32)[None], ones, (slab < slabs - 1).astype(f32)[None]])
    spot = (slab % 2).astype(jnp.int32)[None]
    other = 1 - spot
    own_b = opened(spot, u)
    halo_b = across(own_b)
    own_a = opened(other, u)
    halo_a = beside(own_a)
    taps = pltpu.VMEM((256, 1152), bf16)
    matrix, flipped, offset, diag = run(
        prepare_body,
        "prepare",
        2,
        (taps, taps, pltpu.VMEM((128, 256), f32), pltpu.VMEM((64, 128), f32)),
        [mask, weight, bias[None]],
        scalars=1,
    )
    matrix, flipped, offset, diag = (near(v) for v in (matrix, flipped, offset, diag))
    coarse_shape = pltpu.VMEM((4, 4, 64, 128), bf16)
    average_shape = (4, 4, 64, 128)
    states = (widened(8), widened(6), field(6, f32))
    *kept, lam_rows, average_lam = run(
        inner_body,
        "inner",
        5,
        (*states, coarse_shape, field(4, f32), pltpu.VMEM(average_shape, f32)),
        [spot, near(own_a), near(own_b), lam, matrix, offset],
        [TURN],
        scalars=1,
    )

    def forward(half, kept, halo):
        return run(
            by_half(forward_body),
            "forward",
            4,
            (*states, coarse_shape, field(3, bf16)),
            [half, mask] + [near(v) for v in (*kept, halo, lam_rows)] + [matrix, offset, diag],
            aliases={2: 0, 3: 1, 4: 2, 5: 3},
            scalars=2,
        )

    *kept, own_a = forward(other, kept, halo_a)
    cot_a = beside(own_a)
    wide0, wide1, sens, factor, own_b = forward(spot, kept, halo_b)
    cot_b = across(own_b)
    scale = STEP / math.sqrt(2 * groups * slabs * 4 * 8 * 256)
    back1, back0, middle, blank, blank_sums = run(
        back_inner_body,
        "back_inner",
        3,
        (*states, coarse_shape, pltpu.VMEM((128, 128), f32)),
        [spot] + [near(v) for v in (own_a, own_b, lam_rows, sens)] + [flipped],
        scalars=1,
    )

    def back_outer(half, kept, halo, *after):
        return run(
            by_half(back_outer_body),
            "back_outer",
            3,
            states,
            [half, mask] + [near(v) for v in (*kept, halo, lam_rows, sens)] + [flipped] + [near(v) for v in after],
            aliases={2: 0, 3: 1, 4: 2},
            scalars=2,
        )

    def back_last(half, coarse):
        return run(
            back_last_body,
            "back_last",
            2,
            coarse_shape,
            [half] + [near(v) for v in (back0, middle, average_lam, factor)] + [flipped, near(coarse)],
            aliases={6: 0},
            scalars=1,
        )

    back1, back0, middle = back_outer(other, (back1, back0, middle), cot_a, blank_sums, blank)
    sums_shapes = (pltpu.VMEM((256, 1152), f32), pltpu.VMEM((128, 128), f32))
    total, sums = run(
        gradient_first_body,
        "gradient_first",
        5,
        sums_shapes,
        [spot] + [near(v) for v in (own_a, own_b, wide1, back0, wide0)],
        [pltpu.VMEM((7, 256, 1024), bf16)],
        scalars=1,
    )
    coarse = back_last(other, blank)
    back1, back0, middle = back_outer(spot, (back1, back0, middle), cot_b, sums, coarse)
    half = pltpu.VMEM((8, 64, 128), f32)
    _, _, mine, others = run(
        functools.partial(gradient_last_body, scale),
        "gradient_last",
        2,
        (*sums_shapes, half, half),
        [spot] + [near(v) for v in (back0, wide0, total, sums)],
        [pltpu.VMEM((16, 64, 128), f32), pltpu.VMEM((256, 1024), bf16)],
        aliases={3: 0, 4: 1},
        scalars=1,
    )
    received = beside(others)
    coarse = back_last(spot, coarse)
    pieces = (groups, 128, 128)
    mixed, average_lam = run(
        pack_body,
        "pack",
        1,
        (jax.ShapeDtypeStruct((groups, 320, 128), bf16), jax.ShapeDtypeStruct(average_shape, f32)),
        [near(v) for v in (mine, received, coarse.reshape(pieces), factor.reshape(pieces), average_lam)],
    )
    carried, shared = run(
        meet_body,
        "meet",
        1,
        (jax.ShapeDtypeStruct(pieces, bf16), jax.ShapeDtypeStruct((slabs // 2, 64, 128), bf16)),
        [exchanged(mixed, "tm")],
    )
    same_core = [list(range(core, slabs, 2)) for core in range(2)]
    shared = lax.all_to_all(shared, "slab", 0, 0, tiled=True, axis_index_groups=same_core)
    joined = run(
        join_body,
        "join",
        1,
        jax.ShapeDtypeStruct((groups, 192, 128), bf16),
        [shared, carried],
    )
    joined = exchanged(joined, "tm")
    received = beside(joined[:, 128:])
    updated = run(
        finish_body,
        "finish",
        3,
        jax.ShapeDtypeStruct(lam.shape, f32),
        [lam, average_lam, joined],
        [TURN],
    )
    taps, offset = run(
        taps_body,
        "taps",
        1,
        (jax.ShapeDtypeStruct(weight.shape, f32), jax.ShapeDtypeStruct((1, 64), f32)),
        [spot, joined, received],
        scalars=1,
    )
    return updated[None], taps, offset[0]


def solution(mesh):
    in_specs = (P("tm", None, "slab", None, None), P("tm", None, "slab", None, None), P(), P())
    out_specs = (P("tm", None, "slab", None, None), P(), P())
    return jax.shard_map(
        on_device, mesh=mesh, in_specs=in_specs, out_specs=out_specs, check_vma=False
    )
```

```python
import functools
import math

import jax
import jax.numpy as jnp
from jax import lax
from jax.experimental import pallas as pl
from jax.experimental.pallas import tpu as pltpu
from jax.sharding import PartitionSpec as P

f32, bf16 = jnp.float32, jnp.bfloat16
STEP = 0.25


def shifts(value):
    lane = lax.broadcasted_iota(jnp.int32, value.shape, 1)
    zero = jnp.zeros((), value.dtype)
    left = jnp.where(lane == 0, zero, pltpu.roll(value, 1, 1))
    right = jnp.where(lane == 255, zero, pltpu.roll(value, 255, 1))
    return left, right


def put(wide, plane, row, pair, value):
    count = value.shape[0]
    left, right = shifts(value)
    base = pl.multiple_of(plane * 384 + row, 64)
    cols = slice(pair * 256, pair * 256 + 256)
    wide[pl.ds(base, count), cols] = left
    wide[pl.ds(base + 128, count), cols] = value
    wide[pl.ds(base + 256, count), cols] = right


def to_rows(source, z, turn):
    value = source[:, z].astype(f32).reshape(512, 256)
    turn[0] = value[:, :128]
    turn[1] = value[:, 128:]


def row_of(turn, x):
    return jnp.concatenate([turn[half, pl.ds(x, 64, stride=8), :] for half in range(2)], 1)


def pair_of(turn, pair):
    return jnp.concatenate([row_of(turn, 2 * pair), row_of(turn, 2 * pair + 1)], 0)


def products(matrix, wide, z):
    base = pl.multiple_of(z * 384, 384)
    return [
        jnp.dot(
            matrix[...],
            wide[pl.ds(base, 1152), pair * 256 : pair * 256 + 256],
            preferred_element_type=f32,
        )
        for pair in range(4)
    ]


def combined(parts, pair):
    low, high = parts[pair][0:64], parts[pair][64:128]
    if pair > 0:
        low = low + parts[pair - 1][192:256]
    if pair < 3:
        high = high + parts[pair + 1][128:192]
    return jnp.concatenate([low, high], 0)


def averaging():
    fine = lax.broadcasted_iota(jnp.int32, (256, 128), 0)
    coarse = lax.broadcasted_iota(jnp.int32, (256, 128), 1)
    return jnp.where((fine == 2 * coarse) | (fine == 2 * coarse + 1), 0.25, 0.0).astype(bf16)


def split_dot(value, matrix):
    high = value.astype(bf16)
    low = (value - high.astype(f32)).astype(bf16)
    return jnp.dot(high, matrix, preferred_element_type=f32) + jnp.dot(
        low, matrix, preferred_element_type=f32
    )


def field(planes, dtype):
    return pltpu.VMEM((planes, 128, 1024), dtype)


def widened(planes):
    return pltpu.VMEM((planes * 384, 1024), bf16)


def near(value):
    return pltpu.with_memory_space_constraint(value, pltpu.VMEM)


def run(body, name, micros, outs, ins, scratch=(), aliases=None, scalars=0, limit=8):
    in_specs = [pl.BlockSpec(memory_space=pltpu.SMEM)] * scalars
    in_specs += [pl.BlockSpec(memory_space=pltpu.VMEM)] * (len(ins) - scalars)
    return pl.pallas_call(
        body,
        out_shape=outs,
        in_specs=in_specs,
        scratch_shapes=list(scratch),
        input_output_aliases=aliases or {},
        compiler_params=pltpu.CompilerParams(vmem_limit_bytes=limit * 2**20),
        cost_estimate=pl.CostEstimate(flops=int(micros * 1e8), bytes_accessed=0, transcendentals=0),
        name=name,
    )(*ins)


TURN = pltpu.VMEM((2, 512, 128), f32)


def by_half(body):
    def kernel(half, *refs):
        for known in range(2):
            pl.when(half[0] == known)(functools.partial(body, 2 * known, *refs))

    return kernel


def own_plane(half_b, own_a, own_b, z):
    return jnp.where(half_b[0] == z // 2, own_b[z % 2], own_a[z % 2])


def open_body(half, u, *refs):
    out, planes, turn, arrived = refs[-4:]
    copy = pltpu.make_async_copy(u.at[:, pl.ds(2 * half[0], 2)], planes, arrived)
    copy.start()
    copy.wait()
    for place in range(2):
        to_rows(planes, place, turn)
        for pair in range(4):
            out[place, :, pair * 256 : pair * 256 + 256] = pair_of(turn, pair).astype(bf16)


def opened(half, u, *after):
    return pl.pallas_call(
        open_body,
        out_shape=field(2, bf16),
        in_specs=[pl.BlockSpec(memory_space=pltpu.SMEM)] + [pl.BlockSpec(memory_space=pl.ANY)] * (1 + len(after)),
        scratch_shapes=[pltpu.VMEM((64, 2, 8, 256), bf16), TURN, pltpu.SemaphoreType.DMA(())],
        compiler_params=pltpu.CompilerParams(vmem_limit_bytes=8 * 2**20),
        cost_estimate=pl.CostEstimate(flops=10**8, bytes_accessed=0, transcendentals=0),
        name="open",
    )(half, pltpu.with_memory_space_constraint(u, pltpu.HBM), *after)


def put_plane(wide, z, value):
    for pair in range(4):
        put(wide, z, 0, pair, value[:, pair * 256 : pair * 256 + 256])


def step_state(z, matrix, offset, wide0, wide1, sens, weight):
    parts = products(matrix, wide0, z)
    base = pl.multiple_of((z + 1) * 384, 384)
    for pair in range(4):
        cols = slice(pair * 256, pair * 256 + 256)
        tanh = jnp.tanh(combined(parts, pair) + offset)
        sens[z, :, cols] = 1.0 - tanh * tanh
        value = wide0[pl.ds(base + 128, 128), cols].astype(f32) + STEP * tanh
        if weight is not None:
            value = value * weight
        put(wide1, z, 0, pair, value.astype(bf16))


def inner_body(half_b, own_a, own_b, lam, matrix, bias, wide0, wide1, sens, factor, lam_rows, average_lam, turn):
    average = averaging()
    for z in range(4):
        put_plane(wide0, z + 2, own_plane(half_b, own_a, own_b, z))
    offset = bias[...]

    def inside(z, carry):
        step_state(z, matrix, offset, wide0, wide1, sens, None)
        return carry

    lax.fori_loop(2, 4, inside, 0, unroll=True)
    def lam_plane(z, carry):
        to_rows(lam, z, turn)
        for pair in range(4):
            cols = slice(pair * 256, pair * 256 + 256)
            value = pair_of(turn, pair)
            lam_rows[z, :, cols] = value
            average_lam[z, pair] = split_dot(value[0:64] + value[64:128], average)
        return carry

    lax.fori_loop(0, 4, lam_plane, 0, unroll=True)


def forward_body(base, mask, wide0_in, wide1_in, sens_in, factor_in, halo, lam, matrix, bias, diag, wide0, wide1, sens, factor, cot):
    for place in range(2):
        put_plane(wide0, 3 * base + place, halo[place])
    offset = bias[...]
    for place in range(2):
        z = 2 * base + place
        step_state(z, matrix, offset, wide0, wide1, sens, mask[z])
    average = averaging()
    cot[2] = lam[base + base // 2].astype(bf16)
    for place in range(2):
        z = base + place
        parts = products(matrix, wide1, z)
        for pair in range(4):
            cols = slice(pair * 256, pair * 256 + 256)
            tanh = jnp.tanh(combined(parts, pair) + offset)
            cot[place, :, cols] = ((1.0 - tanh * tanh) * lam[z, :, cols]).astype(bf16)
            both = sens[z + 1, 0:64, cols] + sens[z + 1, 64:128, cols]
            coarse = jnp.dot(both.astype(bf16), average, preferred_element_type=f32)
            factor[z, pair] = (coarse * diag[...]).astype(bf16)


def step_back(z, matrix, wide1, wide0, middle, sens, lam, weight):
    parts = products(matrix, wide1, z)
    for pair in range(4):
        cols = slice(pair * 256, pair * 256 + 256)
        value = lam(cols) + STEP * combined(parts, pair)
        middle[z, :, cols] = value
        value = sens[z, :, cols] * value
        if weight is not None:
            value = value * weight
        put(wide0, z, 0, pair, value.astype(bf16))


def back_inner_body(half_b, own_a, own_b, lam, sens, matrix, wide1, wide0, middle, blank, blank_sums):
    for z in range(4):
        put_plane(wide1, z + 2, own_plane(half_b, own_a, own_b, z))

    def inside(z, carry):
        step_back(z, matrix, wide1, wide0, middle, sens, lambda cols: lam[z - 1, :, cols], None)
        return carry

    lax.fori_loop(2, 4, inside, 0, unroll=True)


def back_outer_body(base, mask, wide1_in, wide0_in, middle_in, halo, lam, sens, matrix, *refs):
    wide1, wide0, middle = refs[-3:]
    for place in range(2):
        put_plane(wide1, 3 * base + place, halo[place])
    z = 1 + base + base // 2
    step_back(z, matrix, wide1, wide0, middle, sens, lambda cols: lam[z - 1, :, cols], None)
    far = 2 * base + base // 2
    step_back(far, matrix, wide1, wide0, middle, sens, lambda cols: halo[2, :, cols].astype(f32), mask[far])


def back_last_body(half, wide0, middle, average_lam, factor, matrix, coarse_in, coarse):
    average = averaging()

    def last(place, carry):
        z = 2 * half[0] + place
        parts = products(matrix, wide0, z)
        for pair in range(4):
            cols = slice(pair * 256, pair * 256 + 256)
            value = middle[z + 1, :, cols] + STEP * combined(parts, pair)
            back = split_dot(value[0:64] + value[64:128], average)
            here = average_lam[z, pair]
            coarse[z, pair] = (back - here - factor[z, pair].astype(f32) * here).astype(bf16)
        return carry

    lax.fori_loop(0, 2, last, 0)


def add_plane(cot, wide, z, widened_cot, total, sums):
    zero = jnp.zeros((64, 256), bf16)
    widened_cot[0:128] = cot
    widened_cot[128:192] = jnp.concatenate([zero, cot[64:128, :768]], 1)
    widened_cot[192:256] = jnp.concatenate([cot[0:64, 256:], zero], 1)
    total[...] += lax.dot_general(
        widened_cot[...],
        wide[pl.ds(pl.multiple_of(z * 384, 384), 1152), :],
        (((1,), (1,)), ((), ())),
        preferred_element_type=f32,
    )
    for part in range(8):
        sums[...] += cot[:, part * 128 : part * 128 + 128].astype(f32)


def centre(back0, z):
    return back0[pl.ds(pl.multiple_of((z + 1) * 384 + 128, 128), 128), :]


def gradient_first_body(half_b, own_a, own_b, wide1, back0, wide0, total, sums, widened_cot):
    total[...] = jnp.zeros_like(total)
    sums[...] = jnp.zeros_like(sums)
    for z in range(4):
        add_plane(own_plane(half_b, own_a, own_b, z), wide1, z, widened_cot.at[z], total, sums)
    for index in range(3):
        z = index + 1 - half_b[0]
        add_plane(centre(back0, z), wide0, z + 1, widened_cot.at[4 + index], total, sums)


def gradient_last_body(scale, spot, back0, wide0, total_in, sums_in, total, sums, mine, others, out, widened_cot):
    z = 3 * spot[0]
    add_plane(centre(back0, z), wide0, z + 1, widened_cot, total, sums)
    lower = lax.broadcasted_iota(jnp.int32, (64, 128), 1) < 64
    for tap in range(9):
        cols = slice(tap * 128, tap * 128 + 128)
        rows = [total[64 * q : 64 * q + 64, cols] * scale for q in range(4)]
        taps = [jnp.where(lower, rows[1], rows[3]), jnp.where(lower, rows[0], rows[1]), jnp.where(lower, rows[2], rows[0])]
        taps = [value + pltpu.roll(value, 64, 1) for value in taps]
        out[tap] = jnp.where(lower, taps[0], taps[1])
        if tap % 2 == 0:
            kept = taps[2]
        else:
            out[9 + tap // 2] = jnp.where(lower, kept, taps[2])
    out[13] = kept
    out[14] = (sums[0:64] + sums[64:128]) * scale
    out[15] = jnp.zeros((64, 128), f32)
    for block in range(8):
        mine[block] = out[block + 8 * spot[0]]
        others[block] = out[block + 8 - 8 * spot[0]]


def pack_body(mine, received, coarse, factor, average_lam, out, kept):
    kept[...] = average_lam[...]
    for group in range(out.shape[0]):
        out[group, 0:128] = coarse[group]
        out[group, 128:256] = factor[group]
        out[group, 256:320] = (mine[group] + received[group]).astype(bf16)


def meet_body(mixed, out, shared):
    groups = mixed.shape[0]
    value = jnp.zeros((128, 128), f32)
    out[0] = value.astype(bf16)
    summed = mixed[0, 256:320].astype(f32)
    for group in range(groups - 1):
        value = value + mixed[group, 128:256].astype(f32) * value + mixed[group, 0:128].astype(f32)
        out[group + 1] = value.astype(bf16)
        summed = summed + mixed[group + 1, 256:320].astype(f32)
    summed = summed.astype(bf16)
    for chip in range(shared.shape[0]):
        shared[chip] = summed


def join_body(shared, carried, out):
    summed = shared[0].astype(f32)
    for chip in range(1, shared.shape[0]):
        summed = summed + shared[chip].astype(f32)
    summed = summed.astype(bf16)
    for group in range(out.shape[0]):
        out[group, 0:128] = carried[group]
        out[group, 128:192] = summed


def finish_body(lam, average_lam, joined, out, turn):
    fine = lax.broadcasted_iota(jnp.int32, (128, 256), 1)
    coarse = lax.broadcasted_iota(jnp.int32, (128, 256), 0)
    copies = jnp.where((fine == 2 * coarse) | (fine == 2 * coarse + 1), 1.0, 0.0).astype(bf16)

    def plane(z, carry):
        for pair in range(4):
            carried = joined[2 * z + pair // 2, 64 * (pair % 2) : 64 * (pair % 2) + 64]
            value = split_dot(carried.astype(f32) - average_lam[z, pair], copies)
            for half in range(2):
                for x in (2 * pair, 2 * pair + 1):
                    turn[half, pl.ds(x, 64, stride=8), :] = value[:, half * 128 : half * 128 + 128]
        added = jnp.concatenate([turn[0], turn[1]], 1).reshape(64, 8, 256)
        out[:, z] = lam[:, z] + added
        return carry

    lax.fori_loop(0, 4, plane, 0, unroll=True)


def taps_body(spot, joined, received, taps, offset):
    def block(index):
        own = joined[index % 8, 128:192].astype(f32)
        other = received[index % 8].astype(f32)
        return jnp.where(spot[0] == index // 8, own, other)

    for a in range(3):
        for c in range(3):
            tap = 3 * a + c
            both = block(tap)
            taps[9 * a + c] = both[:, :64]
            taps[9 * a + 3 + c] = both[:, 64:]
            half = 64 * (tap % 2)
            taps[9 * a + 6 + c] = block(9 + tap // 2)[:, half : half + 64]
    row = lax.broadcasted_iota(jnp.int32, (64, 64), 0)
    col = lax.broadcasted_iota(jnp.int32, (64, 64), 1)
    column = jnp.broadcast_to(jnp.sum(block(14), axis=1, keepdims=True), (64, 64))
    offset[...] = jnp.sum(jnp.where(row == col, column, 0.0), axis=0, keepdims=True)


def prepare_body(mask, weight_in, bias_in, matrix, flipped, offset, diag, weight, bias, arrived):
    copies = [
        pltpu.make_async_copy(source, target, arrived.at[index])
        for index, (source, target) in enumerate(((weight_in, weight), (bias_in, bias)))
    ]
    for copy in copies:
        copy.start()
    for copy in copies:
        copy.wait()
    row = lax.broadcasted_iota(jnp.int32, (64, 64), 0)
    col = lax.broadcasted_iota(jnp.int32, (64, 64), 1)
    zero = jnp.zeros((64, 64), f32)

    def column(values):
        return jnp.sum(jnp.where(row == col, values, 0.0), axis=1, keepdims=True)

    def build(out, tap):
        for a in range(3):
            for c in range(3):
                taps = [tap(9 * a + 3 * b + c) for b in range(3)]
                sides = ((taps[1], taps[2]), (taps[0], taps[1]), (taps[2], zero), (zero, taps[0]))
                start = (3 * a + c) * 128
                for place in range(4):
                    both = jnp.concatenate(sides[place], 1)
                    out[64 * place : 64 * place + 64, start : start + 128] = both.astype(bf16)

    build(matrix, lambda tap: weight[tap].astype(f32))
    build(flipped, lambda tap: weight[26 - tap].astype(f32).T)
    column_bias = jnp.broadcast_to(column(jnp.broadcast_to(bias[...], (64, 64))), (64, 256))
    offset[0:64] = column_bias
    offset[64:128] = column_bias
    diag[...] = jnp.broadcast_to(2.0 * STEP * column(weight[13].astype(f32)), (64, 128))


def beside(value):
    return lax.ppermute(value, "slab", [(i, i ^ 1) for i in range(lax.axis_size("slab"))])


def across(value):
    up = [(i, i + 1) for i in range(1, lax.axis_size("slab") - 1, 2)]
    return lax.ppermute(value, "slab", up + [(j, i) for i, j in up])


def exchanged(value, axes):
    return lax.all_to_all(value, axes, 0, 0, tiled=True)


def on_device(u_states, lam_points, weight, bias):
    u, lam = u_states[0], lam_points[0]
    slab, slabs = lax.axis_index("slab"), lax.axis_size("slab")
    groups = lax.axis_size("tm")
    ones = jnp.ones((4,), f32)
    mask = jnp.concatenate([(slab > 0).astype(f32)[None], ones, (slab < slabs - 1).astype(f32)[None]])
    spot = (slab % 2).astype(jnp.int32)[None]
    other = 1 - spot
    own_b = opened(spot, u)
    halo_b = across(own_b)
    own_a = opened(other, u, own_b)
    halo_a = beside(own_a)
    taps = pltpu.VMEM((256, 1152), bf16)
    matrix, flipped, offset, diag = pl.pallas_call(
        prepare_body,
        out_shape=(taps, taps, pltpu.VMEM((128, 256), f32), pltpu.VMEM((64, 128), f32)),
        in_specs=[pl.BlockSpec(memory_space=pltpu.SMEM)] + [pl.BlockSpec(memory_space=pl.ANY)] * 2,
        scratch_shapes=[
            pltpu.VMEM(weight.shape, bf16),
            pltpu.VMEM((1, 64), f32),
            pltpu.SemaphoreType.DMA((2,)),
        ],
        compiler_params=pltpu.CompilerParams(vmem_limit_bytes=8 * 2**20),
        cost_estimate=pl.CostEstimate(flops=10**8, bytes_accessed=0, transcendentals=0),
        name="prepare",
    )(mask, *(pltpu.with_memory_space_constraint(v, pltpu.HBM) for v in (weight, bias[None])))
    matrix, flipped, offset, diag = (near(v) for v in (matrix, flipped, offset, diag))
    coarse_shape = pltpu.VMEM((4, 4, 64, 128), bf16)
    average_shape = (4, 4, 64, 128)
    states = (widened(8), widened(6), field(6, f32))
    *kept, lam_rows, average_lam = run(
        inner_body,
        "inner",
        5,
        (*states, coarse_shape, field(4, f32), pltpu.VMEM(average_shape, f32)),
        [spot, near(own_a), near(own_b), lam, matrix, offset],
        [TURN],
        scalars=1,
    )

    def forward(half, kept, halo):
        return run(
            by_half(forward_body),
            "forward",
            4,
            (*states, coarse_shape, field(3, bf16)),
            [half, mask] + [near(v) for v in (*kept, halo, lam_rows)] + [matrix, offset, diag],
            aliases={2: 0, 3: 1, 4: 2, 5: 3},
            scalars=2,
        )

    *kept, own_a = forward(other, kept, halo_a)
    cot_a = beside(own_a)
    wide0, wide1, sens, factor, own_b = forward(spot, kept, halo_b)
    cot_b = across(own_b)
    scale = STEP / math.sqrt(2 * groups * slabs * 4 * 8 * 256)
    back1, back0, middle, blank, blank_sums = run(
        back_inner_body,
        "back_inner",
        3,
        (*states, coarse_shape, pltpu.VMEM((128, 128), f32)),
        [spot] + [near(v) for v in (own_a, own_b, lam_rows, sens)] + [flipped],
        scalars=1,
    )

    def back_outer(half, kept, halo, *after):
        return run(
            by_half(back_outer_body),
            "back_outer",
            3,
            states,
            [half, mask] + [near(v) for v in (*kept, halo, lam_rows, sens)] + [flipped] + [near(v) for v in after],
            aliases={2: 0, 3: 1, 4: 2},
            scalars=2,
        )

    def back_last(half, coarse):
        return run(
            back_last_body,
            "back_last",
            2,
            coarse_shape,
            [half] + [near(v) for v in (back0, middle, average_lam, factor)] + [flipped, near(coarse)],
            aliases={6: 0},
            scalars=1,
        )

    back1, back0, middle = back_outer(other, (back1, back0, middle), cot_a, blank_sums, blank)
    sums_shapes = (pltpu.VMEM((256, 1152), f32), pltpu.VMEM((128, 128), f32))
    total, sums = run(
        gradient_first_body,
        "gradient_first",
        5,
        sums_shapes,
        [spot] + [near(v) for v in (own_a, own_b, wide1, back0, wide0)],
        [pltpu.VMEM((7, 256, 1024), bf16)],
        scalars=1,
    )
    coarse = back_last(other, blank)
    back1, back0, middle = back_outer(spot, (back1, back0, middle), cot_b, sums, coarse)
    half = pltpu.VMEM((8, 64, 128), f32)
    _, _, mine, others = run(
        functools.partial(gradient_last_body, scale),
        "gradient_last",
        2,
        (*sums_shapes, half, half),
        [spot] + [near(v) for v in (back0, wide0, total, sums)],
        [pltpu.VMEM((16, 64, 128), f32), pltpu.VMEM((256, 1024), bf16)],
        aliases={3: 0, 4: 1},
        scalars=1,
    )
    received = beside(others)
    coarse = back_last(spot, coarse)
    pieces = (groups, 128, 128)
    mixed, average_lam = run(
        pack_body,
        "pack",
        1,
        (jax.ShapeDtypeStruct((groups, 320, 128), bf16), jax.ShapeDtypeStruct(average_shape, f32)),
        [near(v) for v in (mine, received, coarse.reshape(pieces), factor.reshape(pieces), average_lam)],
    )
    carried, shared = run(
        meet_body,
        "meet",
        1,
        (jax.ShapeDtypeStruct(pieces, bf16), jax.ShapeDtypeStruct((slabs // 2, 64, 128), bf16)),
        [exchanged(mixed, "tm")],
    )
    same_core = [list(range(core, slabs, 2)) for core in range(2)]
    shared = lax.all_to_all(shared, "slab", 0, 0, tiled=True, axis_index_groups=same_core)
    joined = run(
        join_body,
        "join",
        1,
        jax.ShapeDtypeStruct((groups, 192, 128), bf16),
        [shared, carried],
    )
    joined = exchanged(joined, "tm")
    received = beside(joined[:, 128:])
    updated = run(
        finish_body,
        "finish",
        3,
        jax.ShapeDtypeStruct(lam.shape, f32),
        [lam, average_lam, joined],
        [TURN],
    )
    taps, offset = run(
        taps_body,
        "taps",
        1,
        (jax.ShapeDtypeStruct(weight.shape, f32), jax.ShapeDtypeStruct((1, 64), f32)),
        [spot, joined, received],
        scalars=1,
    )
    return updated[None], taps, offset[0]


def solution(mesh):
    in_specs = (P("tm", None, "slab", None, None), P("tm", None, "slab", None, None), P(), P())
    out_specs = (P("tm", None, "slab", None, None), P(), P())
    return jax.shard_map(
        on_device, mesh=mesh, in_specs=in_specs, out_specs=out_specs, check_vma=False
    )
```

```python
import functools
import math

import jax
import jax.numpy as jnp
from jax import lax
from jax.experimental import pallas as pl
from jax.experimental.pallas import tpu as pltpu
from jax.sharding import PartitionSpec as P

f32, bf16 = jnp.float32, jnp.bfloat16
STEP = 0.25


def shifts(value):
    lane = lax.broadcasted_iota(jnp.int32, value.shape, 1)
    zero = jnp.zeros((), value.dtype)
    left = jnp.where(lane == 0, zero, pltpu.roll(value, 1, 1))
    right = jnp.where(lane == 255, zero, pltpu.roll(value, 255, 1))
    return left, right


def put(wide, plane, row, pair, value):
    count = value.shape[0]
    left, right = shifts(value)
    base = pl.multiple_of(plane * 384 + row, 64)
    cols = slice(pair * 256, pair * 256 + 256)
    wide[pl.ds(base, count), cols] = left
    wide[pl.ds(base + 128, count), cols] = value
    wide[pl.ds(base + 256, count), cols] = right


def to_rows(source, z, turn):
    value = source[:, z].astype(f32).reshape(512, 256)
    turn[0] = value[:, :128]
    turn[1] = value[:, 128:]


def row_of(turn, x):
    return jnp.concatenate([turn[half, pl.ds(x, 64, stride=8), :] for half in range(2)], 1)


def pair_of(turn, pair):
    return jnp.concatenate([row_of(turn, 2 * pair), row_of(turn, 2 * pair + 1)], 0)


def products(matrix, wide, z):
    base = pl.multiple_of(z * 384, 384)
    return [
        jnp.dot(
            matrix[...],
            wide[pl.ds(base, 1152), pair * 256 : pair * 256 + 256],
            preferred_element_type=f32,
        )
        for pair in range(4)
    ]


def combined(parts, pair):
    low, high = parts[pair][0:64], parts[pair][64:128]
    if pair > 0:
        low = low + parts[pair - 1][192:256]
    if pair < 3:
        high = high + parts[pair + 1][128:192]
    return jnp.concatenate([low, high], 0)


def averaging():
    fine = lax.broadcasted_iota(jnp.int32, (256, 128), 0)
    coarse = lax.broadcasted_iota(jnp.int32, (256, 128), 1)
    return jnp.where((fine == 2 * coarse) | (fine == 2 * coarse + 1), 0.25, 0.0).astype(bf16)


def split_dot(value, matrix):
    high = value.astype(bf16)
    low = (value - high.astype(f32)).astype(bf16)
    return jnp.dot(high, matrix, preferred_element_type=f32) + jnp.dot(
        low, matrix, preferred_element_type=f32
    )


def field(planes, dtype):
    return pltpu.VMEM((planes, 128, 1024), dtype)


def widened(planes):
    return pltpu.VMEM((planes * 384, 1024), bf16)


def near(value):
    return pltpu.with_memory_space_constraint(value, pltpu.VMEM)


def run(body, name, micros, outs, ins, scratch=(), aliases=None, scalars=0, limit=8):
    in_specs = [pl.BlockSpec(memory_space=pltpu.SMEM)] * scalars
    in_specs += [pl.BlockSpec(memory_space=pltpu.VMEM)] * (len(ins) - scalars)
    return pl.pallas_call(
        body,
        out_shape=outs,
        in_specs=in_specs,
        scratch_shapes=list(scratch),
        input_output_aliases=aliases or {},
        compiler_params=pltpu.CompilerParams(vmem_limit_bytes=limit * 2**20),
        cost_estimate=pl.CostEstimate(flops=int(micros * 1e8), bytes_accessed=0, transcendentals=0),
        name=name,
    )(*ins)


TURN = pltpu.VMEM((2, 512, 128), f32)


def by_half(body):
    def kernel(half, *refs):
        for known in range(2):
            pl.when(half[0] == known)(functools.partial(body, 2 * known, *refs))

    return kernel


def own_plane(half_b, own_a, own_b, z):
    return jnp.where(half_b[0] == z // 2, own_b[z % 2], own_a[z % 2])


def open_body(half, u, *refs):
    out, planes, turn, arrived = refs[-4:]
    copy = pltpu.make_async_copy(u.at[:, pl.ds(2 * half[0], 2)], planes, arrived)
    copy.start()
    copy.wait()
    for place in range(2):
        to_rows(planes, place, turn)
        for pair in range(4):
            out[place, :, pair * 256 : pair * 256 + 256] = pair_of(turn, pair).astype(bf16)


def opened(half, u, *after):
    return pl.pallas_call(
        open_body,
        out_shape=field(2, bf16),
        in_specs=[pl.BlockSpec(memory_space=pltpu.SMEM)] + [pl.BlockSpec(memory_space=pl.ANY)] * (1 + len(after)),
        scratch_shapes=[pltpu.VMEM((64, 2, 8, 256), bf16), TURN, pltpu.SemaphoreType.DMA(())],
        compiler_params=pltpu.CompilerParams(vmem_limit_bytes=8 * 2**20),
        cost_estimate=pl.CostEstimate(flops=10**8, bytes_accessed=0, transcendentals=0),
        name="open",
    )(half, pltpu.with_memory_space_constraint(u, pltpu.HBM), *after)


def put_plane(wide, z, value):
    for pair in range(4):
        put(wide, z, 0, pair, value[:, pair * 256 : pair * 256 + 256])


def step_state(z, matrix, offset, wide0, wide1, sens, weight):
    parts = products(matrix, wide0, z)
    base = pl.multiple_of((z + 1) * 384, 384)
    for pair in range(4):
        cols = slice(pair * 256, pair * 256 + 256)
        tanh = jnp.tanh(combined(parts, pair) + offset)
        sens[z, :, cols] = 1.0 - tanh * tanh
        value = wide0[pl.ds(base + 128, 128), cols].astype(f32) + STEP * tanh
        if weight is not None:
            value = value * weight
        put(wide1, z, 0, pair, value.astype(bf16))


def inner_body(half_b, own_a, own_b, lam, matrix, bias, wide0, wide1, sens, factor, lam_rows, average_lam, turn):
    average = averaging()
    for z in range(4):
        put_plane(wide0, z + 2, own_plane(half_b, own_a, own_b, z))
    offset = bias[...]

    def inside(z, carry):
        step_state(z, matrix, offset, wide0, wide1, sens, None)
        return carry

    lax.fori_loop(2, 4, inside, 0, unroll=True)
    def lam_plane(z, carry):
        to_rows(lam, z, turn)
        for pair in range(4):
            cols = slice(pair * 256, pair * 256 + 256)
            value = pair_of(turn, pair)
            lam_rows[z, :, cols] = value
            average_lam[z, pair] = split_dot(value[0:64] + value[64:128], average)
        return carry

    lax.fori_loop(0, 4, lam_plane, 0, unroll=True)


def forward_body(base, mask, wide0_in, wide1_in, sens_in, factor_in, halo, lam, matrix, bias, diag, wide0, wide1, sens, factor, cot):
    for place in range(2):
        put_plane(wide0, 3 * base + place, halo[place])
    offset = bias[...]
    for place in range(2):
        z = 2 * base + place
        step_state(z, matrix, offset, wide0, wide1, sens, mask[z])
    average = averaging()
    cot[2] = lam[base + base // 2].astype(bf16)
    for place in range(2):
        z = base + place
        parts = products(matrix, wide1, z)
        for pair in range(4):
            cols = slice(pair * 256, pair * 256 + 256)
            tanh = jnp.tanh(combined(parts, pair) + offset)
            cot[place, :, cols] = ((1.0 - tanh * tanh) * lam[z, :, cols]).astype(bf16)
            both = sens[z + 1, 0:64, cols] + sens[z + 1, 64:128, cols]
            coarse = jnp.dot(both.astype(bf16), average, preferred_element_type=f32)
            factor[z, pair] = (coarse * diag[...]).astype(bf16)


def step_back(z, matrix, wide1, wide0, middle, sens, lam, weight):
    parts = products(matrix, wide1, z)
    for pair in range(4):
        cols = slice(pair * 256, pair * 256 + 256)
        value = lam(cols) + STEP * combined(parts, pair)
        middle[z, :, cols] = value
        value = sens[z, :, cols] * value
        if weight is not None:
            value = value * weight
        put(wide0, z, 0, pair, value.astype(bf16))


def back_inner_body(half_b, own_a, own_b, lam, sens, matrix, wide1, wide0, middle, blank, blank_sums):
    for z in range(4):
        put_plane(wide1, z + 2, own_plane(half_b, own_a, own_b, z))

    def inside(z, carry):
        step_back(z, matrix, wide1, wide0, middle, sens, lambda cols: lam[z - 1, :, cols], None)
        return carry

    lax.fori_loop(2, 4, inside, 0, unroll=True)


def back_outer_body(base, mask, wide1_in, wide0_in, middle_in, halo, lam, sens, matrix, *refs):
    wide1, wide0, middle = refs[-3:]
    for place in range(2):
        put_plane(wide1, 3 * base + place, halo[place])
    z = 1 + base + base // 2
    step_back(z, matrix, wide1, wide0, middle, sens, lambda cols: lam[z - 1, :, cols], None)
    far = 2 * base + base // 2
    step_back(far, matrix, wide1, wide0, middle, sens, lambda cols: halo[2, :, cols].astype(f32), mask[far])


def back_last_body(half, wide0, middle, average_lam, factor, matrix, coarse_in, coarse):
    average = averaging()

    def last(place, carry):
        z = 2 * half[0] + place
        parts = products(matrix, wide0, z)
        for pair in range(4):
            cols = slice(pair * 256, pair * 256 + 256)
            value = middle[z + 1, :, cols] + STEP * combined(parts, pair)
            back = split_dot(value[0:64] + value[64:128], average)
            here = average_lam[z, pair]
            coarse[z, pair] = (back - here - factor[z, pair].astype(f32) * here).astype(bf16)
        return carry

    lax.fori_loop(0, 2, last, 0)


def add_plane(cot, wide, z, widened_cot, total, sums):
    zero = jnp.zeros((64, 256), bf16)
    widened_cot[0:128] = cot
    widened_cot[128:192] = jnp.concatenate([zero, cot[64:128, :768]], 1)
    widened_cot[192:256] = jnp.concatenate([cot[0:64, 256:], zero], 1)
    total[...] += lax.dot_general(
        widened_cot[...],
        wide[pl.ds(pl.multiple_of(z * 384, 384), 1152), :],
        (((1,), (1,)), ((), ())),
        preferred_element_type=f32,
    )
    for part in range(8):
        sums[...] += cot[:, part * 128 : part * 128 + 128].astype(f32)


def centre(back0, z):
    return back0[pl.ds(pl.multiple_of((z + 1) * 384 + 128, 128), 128), :]


def gradient_first_body(half_b, own_a, own_b, wide1, back0, wide0, total, sums, widened_cot):
    total[...] = jnp.zeros_like(total)
    sums[...] = jnp.zeros_like(sums)
    for z in range(4):
        add_plane(own_plane(half_b, own_a, own_b, z), wide1, z, widened_cot.at[z], total, sums)
    for index in range(3):
        z = index + 1 - half_b[0]
        add_plane(centre(back0, z), wide0, z + 1, widened_cot.at[4 + index], total, sums)


def gradient_last_body(scale, spot, back0, wide0, total_in, sums_in, total, sums, mine, others, out, widened_cot):
    z = 3 * spot[0]
    add_plane(centre(back0, z), wide0, z + 1, widened_cot, total, sums)
    lower = lax.broadcasted_iota(jnp.int32, (64, 128), 1) < 64
    for tap in range(9):
        cols = slice(tap * 128, tap * 128 + 128)
        rows = [total[64 * q : 64 * q + 64, cols] * scale for q in range(4)]
        taps = [jnp.where(lower, rows[1], rows[3]), jnp.where(lower, rows[0], rows[1]), jnp.where(lower, rows[2], rows[0])]
        taps = [value + pltpu.roll(value, 64, 1) for value in taps]
        out[tap] = jnp.where(lower, taps[0], taps[1])
        if tap % 2 == 0:
            kept = taps[2]
        else:
            out[9 + tap // 2] = jnp.where(lower, kept, taps[2])
    out[13] = kept
    out[14] = (sums[0:64] + sums[64:128]) * scale
    out[15] = jnp.zeros((64, 128), f32)
    for block in range(8):
        mine[block] = out[block + 8 * spot[0]]
        others[block] = out[block + 8 - 8 * spot[0]]


def pack_body(mine, received, coarse, factor, average_lam, out, kept):
    kept[...] = average_lam[...]
    for group in range(out.shape[0]):
        out[group, 0:128] = coarse[group]
        out[group, 128:256] = factor[group]
        out[group, 256:320] = (mine[group] + received[group]).astype(bf16)


def meet_body(mixed, out, shared):
    groups = mixed.shape[0]
    value = jnp.zeros((128, 128), f32)
    out[0] = value.astype(bf16)
    summed = mixed[0, 256:320].astype(f32)
    for group in range(groups - 1):
        value = value + mixed[group, 128:256].astype(f32) * value + mixed[group, 0:128].astype(f32)
        out[group + 1] = value.astype(bf16)
        summed = summed + mixed[group + 1, 256:320].astype(f32)
    summed = summed.astype(bf16)
    for chip in range(shared.shape[0]):
        shared[chip] = summed


def join_body(shared, carried, out):
    summed = shared[0].astype(f32)
    for chip in range(1, shared.shape[0]):
        summed = summed + shared[chip].astype(f32)
    summed = summed.astype(bf16)
    for group in range(out.shape[0]):
        out[group, 0:128] = carried[group]
        out[group, 128:192] = summed


def finish_body(lam, average_lam, joined, out, turn):
    fine = lax.broadcasted_iota(jnp.int32, (128, 256), 1)
    coarse = lax.broadcasted_iota(jnp.int32, (128, 256), 0)
    copies = jnp.where((fine == 2 * coarse) | (fine == 2 * coarse + 1), 1.0, 0.0).astype(bf16)

    def plane(z, carry):
        for pair in range(4):
            carried = joined[2 * z + pair // 2, 64 * (pair % 2) : 64 * (pair % 2) + 64]
            value = split_dot(carried.astype(f32) - average_lam[z, pair], copies)
            for half in range(2):
                for x in (2 * pair, 2 * pair + 1):
                    turn[half, pl.ds(x, 64, stride=8), :] = value[:, half * 128 : half * 128 + 128]
        added = jnp.concatenate([turn[0], turn[1]], 1).reshape(64, 8, 256)
        out[:, z] = lam[:, z] + added
        return carry

    lax.fori_loop(0, 4, plane, 0, unroll=True)


def taps_body(spot, joined, received, taps, offset):
    def block(index):
        own = joined[index % 8, 128:192].astype(f32)
        other = received[index % 8].astype(f32)
        return jnp.where(spot[0] == index // 8, own, other)

    for a in range(3):
        for c in range(3):
            tap = 3 * a + c
            both = block(tap)
            taps[9 * a + c] = both[:, :64]
            taps[9 * a + 3 + c] = both[:, 64:]
            half = 64 * (tap % 2)
            taps[9 * a + 6 + c] = block(9 + tap // 2)[:, half : half + 64]
    row = lax.broadcasted_iota(jnp.int32, (64, 64), 0)
    col = lax.broadcasted_iota(jnp.int32, (64, 64), 1)
    column = jnp.broadcast_to(jnp.sum(block(14), axis=1, keepdims=True), (64, 64))
    offset[...] = jnp.sum(jnp.where(row == col, column, 0.0), axis=0, keepdims=True)


def prepare_body(half, mask, u, weight_in, bias_in, own_b, own_a, matrix, flipped, offset, diag, planes, turn, weight, bias, arrived):
    copies = [
        pltpu.make_async_copy(source, target, arrived.at[index])
        for index, (source, target) in enumerate(
            ((u.at[:, pl.ds(2 * half[0], 2)], planes), (weight_in, weight), (bias_in, bias))
        )
    ]
    for copy in copies:
        copy.start()
    copies[0].wait()
    for place in range(2):
        to_rows(planes, place, turn)
        for pair in range(4):
            own_a[place, :, pair * 256 : pair * 256 + 256] = pair_of(turn, pair).astype(bf16)
    for copy in copies[1:]:
        copy.wait()
    row = lax.broadcasted_iota(jnp.int32, (64, 64), 0)
    col = lax.broadcasted_iota(jnp.int32, (64, 64), 1)
    zero = jnp.zeros((64, 64), f32)

    def column(values):
        return jnp.sum(jnp.where(row == col, values, 0.0), axis=1, keepdims=True)

    def build(out, tap):
        for a in range(3):
            for c in range(3):
                taps = [tap(9 * a + 3 * b + c) for b in range(3)]
                sides = ((taps[1], taps[2]), (taps[0], taps[1]), (taps[2], zero), (zero, taps[0]))
                start = (3 * a + c) * 128
                for place in range(4):
                    both = jnp.concatenate(sides[place], 1)
                    out[64 * place : 64 * place + 64, start : start + 128] = both.astype(bf16)

    build(matrix, lambda tap: weight[tap].astype(f32))
    build(flipped, lambda tap: weight[26 - tap].astype(f32).T)
    column_bias = jnp.broadcast_to(column(jnp.broadcast_to(bias[...], (64, 64))), (64, 256))
    offset[0:64] = column_bias
    offset[64:128] = column_bias
    diag[...] = jnp.broadcast_to(2.0 * STEP * column(weight[13].astype(f32)), (64, 128))


def beside(value):
    return lax.ppermute(value, "slab", [(i, i ^ 1) for i in range(lax.axis_size("slab"))])


def across(value):
    up = [(i, i + 1) for i in range(1, lax.axis_size("slab") - 1, 2)]
    return lax.ppermute(value, "slab", up + [(j, i) for i, j in up])


def exchanged(value, axes):
    return lax.all_to_all(value, axes, 0, 0, tiled=True)


def on_device(u_states, lam_points, weight, bias):
    u, lam = u_states[0], lam_points[0]
    slab, slabs = lax.axis_index("slab"), lax.axis_size("slab")
    groups = lax.axis_size("tm")
    ones = jnp.ones((4,), f32)
    mask = jnp.concatenate([(slab > 0).astype(f32)[None], ones, (slab < slabs - 1).astype(f32)[None]])
    spot = (slab % 2).astype(jnp.int32)[None]
    other = 1 - spot
    own_b = opened(spot, u)
    halo_b = across(own_b)
    taps = pltpu.VMEM((256, 1152), bf16)
    own_a, matrix, flipped, offset, diag = pl.pallas_call(
        prepare_body,
        out_shape=(field(2, bf16), taps, taps, pltpu.VMEM((128, 256), f32), pltpu.VMEM((64, 128), f32)),
        in_specs=[pl.BlockSpec(memory_space=pltpu.SMEM)] * 2 + [pl.BlockSpec(memory_space=pl.ANY)] * 4,
        scratch_shapes=[
            pltpu.VMEM((64, 2, 8, 256), bf16),
            TURN,
            pltpu.VMEM(weight.shape, bf16),
            pltpu.VMEM((1, 64), f32),
            pltpu.SemaphoreType.DMA((3,)),
        ],
        compiler_params=pltpu.CompilerParams(vmem_limit_bytes=8 * 2**20),
        cost_estimate=pl.CostEstimate(flops=10**8, bytes_accessed=0, transcendentals=0),
        name="prepare",
    )(other, mask, *(pltpu.with_memory_space_constraint(v, pltpu.HBM) for v in (u, weight, bias[None])), own_b)
    halo_a = beside(own_a)
    matrix, flipped, offset, diag = (near(v) for v in (matrix, flipped, offset, diag))
    coarse_shape = pltpu.VMEM((4, 4, 64, 128), bf16)
    average_shape = (4, 4, 64, 128)
    states = (widened(8), widened(6), field(6, f32))
    *kept, lam_rows, average_lam = run(
        inner_body,
        "inner",
        5,
        (*states, coarse_shape, field(4, f32), pltpu.VMEM(average_shape, f32)),
        [spot, near(own_a), near(own_b), lam, matrix, offset],
        [TURN],
        scalars=1,
    )

    def forward(half, kept, halo):
        return run(
            by_half(forward_body),
            "forward",
            4,
            (*states, coarse_shape, field(3, bf16)),
            [half, mask] + [near(v) for v in (*kept, halo, lam_rows)] + [matrix, offset, diag],
            aliases={2: 0, 3: 1, 4: 2, 5: 3},
            scalars=2,
        )

    *kept, own_a = forward(other, kept, halo_a)
    cot_a = beside(own_a)
    wide0, wide1, sens, factor, own_b = forward(spot, kept, halo_b)
    cot_b = across(own_b)
    scale = STEP / math.sqrt(2 * groups * slabs * 4 * 8 * 256)
    back1, back0, middle, blank, blank_sums = run(
        back_inner_body,
        "back_inner",
        3,
        (*states, coarse_shape, pltpu.VMEM((128, 128), f32)),
        [spot] + [near(v) for v in (own_a, own_b, lam_rows, sens)] + [flipped],
        scalars=1,
    )

    def back_outer(half, kept, halo, *after):
        return run(
            by_half(back_outer_body),
            "back_outer",
            3,
            states,
            [half, mask] + [near(v) for v in (*kept, halo, lam_rows, sens)] + [flipped] + [near(v) for v in after],
            aliases={2: 0, 3: 1, 4: 2},
            scalars=2,
        )

    def back_last(half, coarse):
        return run(
            back_last_body,
            "back_last",
            2,
            coarse_shape,
            [half] + [near(v) for v in (back0, middle, average_lam, factor)] + [flipped, near(coarse)],
            aliases={6: 0},
            scalars=1,
        )

    back1, back0, middle = back_outer(other, (back1, back0, middle), cot_a, blank_sums, blank)
    sums_shapes = (pltpu.VMEM((256, 1152), f32), pltpu.VMEM((128, 128), f32))
    total, sums = run(
        gradient_first_body,
        "gradient_first",
        5,
        sums_shapes,
        [spot] + [near(v) for v in (own_a, own_b, wide1, back0, wide0)],
        [pltpu.VMEM((7, 256, 1024), bf16)],
        scalars=1,
    )
    coarse = back_last(other, blank)
    back1, back0, middle = back_outer(spot, (back1, back0, middle), cot_b, sums, coarse)
    half = pltpu.VMEM((8, 64, 128), f32)
    _, _, mine, others = run(
        functools.partial(gradient_last_body, scale),
        "gradient_last",
        2,
        (*sums_shapes, half, half),
        [spot] + [near(v) for v in (back0, wide0, total, sums)],
        [pltpu.VMEM((16, 64, 128), f32), pltpu.VMEM((256, 1024), bf16)],
        aliases={3: 0, 4: 1},
        scalars=1,
    )
    received = beside(others)
    coarse = back_last(spot, coarse)
    pieces = (groups, 128, 128)
    mixed, average_lam = run(
        pack_body,
        "pack",
        1,
        (jax.ShapeDtypeStruct((groups, 320, 128), bf16), jax.ShapeDtypeStruct(average_shape, f32)),
        [near(v) for v in (mine, received, coarse.reshape(pieces), factor.reshape(pieces), average_lam)],
    )
    carried, shared = run(
        meet_body,
        "meet",
        1,
        (jax.ShapeDtypeStruct(pieces, bf16), jax.ShapeDtypeStruct((slabs // 2, 64, 128), bf16)),
        [exchanged(mixed, "tm")],
    )
    same_core = [list(range(core, slabs, 2)) for core in range(2)]
    shared = lax.all_to_all(shared, "slab", 0, 0, tiled=True, axis_index_groups=same_core)
    joined = run(
        join_body,
        "join",
        1,
        jax.ShapeDtypeStruct((groups, 192, 128), bf16),
        [shared, carried],
    )
    joined = exchanged(joined, "tm")
    received = beside(joined[:, 128:])
    updated = run(
        finish_body,
        "finish",
        3,
        jax.ShapeDtypeStruct(lam.shape, f32),
        [lam, average_lam, joined],
        [TURN],
    )
    taps, offset = run(
        taps_body,
        "taps",
        1,
        (jax.ShapeDtypeStruct(weight.shape, f32), jax.ShapeDtypeStruct((1, 64), f32)),
        [spot, joined, received],
        scalars=1,
    )
    return updated[None], taps, offset[0]


def solution(mesh):
    in_specs = (P("tm", None, "slab", None, None), P("tm", None, "slab", None, None), P(), P())
    out_specs = (P("tm", None, "slab", None, None), P(), P())
    return jax.shard_map(
        on_device, mesh=mesh, in_specs=in_specs, out_specs=out_specs, check_vma=False
    )
```
